128 devices in a mesh: leaf: 128 (over x, y, z, core).
Axes of the slice: x: 4, y: 4, z: 4, core: 2. Of those that a mesh axis runs over, the one named last changes fastest.
Arguments:
- right_sides: bfloat16 [524288, 128], P('leaf'), may hold values from -6 to 6
- coords: float32 [3, 524288], P(None, 'leaf'), may hold values from 0 to 1
- cluster_order: int32 [128, 4096], P('leaf'), may hold values from 0 to 4095, each once within a row
- bases: bfloat16 [7, 64, 524288], P(None, None, 'leaf'), may hold values from -5 to 5
- coupling: float32 [127, 64, 64], replicated, may hold values from -0.75 to 0.75
Outputs:
- product: float32 [524288, 128], P('leaf')
The draws below stay inside these ranges and needn't reach their ends.
Inputs may be any that keep to these rules, and one draw needn't show every extreme that they name: `cluster_order`: each row lists every one of a leaf's 4096 points once.
All inputs are finite; a program needn't handle non-finite values.
Results may differ from the reference program's by a relative error of at most 0.0029.
Values sent between devices are 32-bit elements; how exact they have to be, the bound alone decides.
No kernel may reach another device: no remote copies, remote signals or barrier semaphores. Data moves between devices by JAX's collectives and lax.ppermute only.
A program may use at most 128 MiB of HBM per device.

```python
import math
import jax
import jax.numpy as jnp
from jax import lax

LEAF = 4096
RANK = 64
NRHS = 128
LEVELS = 7
POINTS = 524288
N_LEAF = 128


def shard_levels(key, shape, split, least, largest):
    factor_of, own = 1.0, jax.random.fold_in(key, 6)
    for position, parts in split:
        heights = jnp.exp(jax.random.uniform(jax.random.fold_in(own, position), (parts,), jnp.float32, least / len(split), largest / len(split)))
        factor_of = factor_of * jnp.repeat(heights, shape[position] // parts).reshape([-1 if axis == position else 1 for axis in range(len(shape))])
    return factor_of


def centred(key, shape, spread, reach, shards=(), kind=jnp.bfloat16):
    result = spread * jax.random.normal(key, shape, jnp.float32)
    if shards:
        result = result * shard_levels(key, shape, shards, -0.22, 0.18)
    return jnp.clip(result, -reach, reach).astype(kind)


def setup_inputs(seed: int = 0) -> dict:
    key_of = jax.random.split(jax.random.key(seed), 6)
    right_sides = centred(key_of[0], (POINTS, NRHS), 1.0, 6.0, ((0, 128),))
    coords = jnp.clip(1.0 * jax.random.uniform(key_of[1], (3, POINTS), jnp.float32) ** shard_levels(key_of[1], (3, POINTS), ((1, 128),), -0.2, 0.2), 0.0, 1.0)
    cluster_order = jax.vmap(lambda own: jax.random.permutation(own, LEAF))(jax.random.split(key_of[2], N_LEAF)).reshape((N_LEAF, LEAF)).astype(jnp.int32)
    bases = centred(key_of[3], (LEVELS, RANK, POINTS), 0.35, 5.0, ((2, 128),))
    coupling = centred(key_of[4], (N_LEAF - 1, RANK, RANK), RANK ** -0.5, 0.75, (), jnp.float32)
    return {"right_sides": right_sides, "coords": coords, "cluster_order": cluster_order, "bases": bases, "coupling": coupling}


length_scale = 0.25
kernel_amplitude = 0.25
root_three = math.sqrt(3.0)

def matern_rows(row_points, all_points):
    squared = jnp.zeros((row_points.shape[1], all_points.shape[1]), jnp.float32)
    for coord_index in range(3):
        differ = row_points[coord_index][:, None] - all_points[coord_index][None, :]
        squared = squared + differ * differ
    scaled = root_three * jnp.sqrt(squared) / length_scale
    return (kernel_amplitude * (1.0 + scaled) * jnp.exp(-scaled)).astype(jnp.bfloat16)

def leaf_product(points, values):
    leaf_count = values.shape[0]
    block_rows = min(512, leaf_count)
    starts = jnp.arange(leaf_count // block_rows, dtype=jnp.int32) * block_rows

    def one_block(start):
        rows = lax.dynamic_slice_in_dim(points, start, block_rows, 1)
        kernel = matern_rows(rows, points)
        return jnp.dot(kernel, values, preferred_element_type=jnp.float32)
    return lax.map(one_block, starts).reshape(leaf_count, values.shape[1])

def reference(right_sides, coords, cluster_order, bases, coupling):
    leaves = N_LEAF
    values = right_sides.reshape(leaves, LEAF, NRHS)
    values = jnp.take_along_axis(values, cluster_order[:, :, None], axis=1)
    points = coords.reshape(3, leaves, LEAF)
    points = jnp.take_along_axis(points, cluster_order[None, :, :], axis=2)
    points = jnp.transpose(points, (1, 0, 2))
    total = lax.map(lambda pair: leaf_product(pair[0], pair[1]), (points, values))
    values_wide = values.astype(jnp.float32)
    for level_no in range(LEVELS):
        group = 2 ** level_no
        pairs = leaves // (2 * group)
        basis = bases[level_no].reshape(RANK, leaves, LEAF).astype(jnp.float32)
        projected = jnp.einsum('rkp,kpn->krn', basis, values_wide)
        grouped = projected.reshape(pairs, 2, group, RANK, NRHS).sum(axis=2) * (1.0 / math.sqrt(group * LEAF))
        matrices = coupling[pairs - 1:2 * pairs - 1]
        first_side = jnp.einsum('prs,psn->prn', matrices, grouped[:, 1], precision=lax.Precision.HIGHEST)
        second_side = jnp.einsum('psr,psn->prn', matrices, grouped[:, 0], precision=lax.Precision.HIGHEST)
        mixed = jnp.stack([first_side, second_side], axis=1)
        mixed = jnp.broadcast_to(mixed[:, :, None], (pairs, 2, group, RANK, NRHS)).reshape(leaves, RANK, NRHS)
        mixed = mixed.astype(jnp.bfloat16)
        total = total + jnp.einsum('rkp,krn->kpn', basis, mixed.astype(jnp.float32))
    leaf_ids = jnp.arange(leaves, dtype=jnp.int32)[:, None]
    placed = jnp.zeros((leaves, LEAF, NRHS), jnp.float32).at[leaf_ids, cluster_order].set(total)
    return placed.reshape(leaves * LEAF, NRHS)
```

```python
import functools
import math

import jax
import jax.numpy as jnp
from jax import lax
from jax.experimental import pallas as pl
from jax.experimental.pallas import tpu as pltpu
from jax.sharding import PartitionSpec as P

length_scale = 0.25
kernel_amplitude = 0.25
root_three = math.sqrt(3.0)
log_two = math.log(2.0)
point_scale = root_three / length_scale / log_two
block = 256
group_tiles = 4
feature_rows = 32
unroll = 16
near_shares = (4, 3, 3, 2, 2, 2)
partner_masks = (1, 2, 6, 8, 24, 32, 96)

vmem = pl.BlockSpec(memory_space=pltpu.VMEM)
smem = pl.BlockSpec(memory_space=pltpu.SMEM)
f32, bf16 = jnp.float32, jnp.bfloat16


def params(mib):
    return pltpu.CompilerParams(vmem_limit_bytes=mib * 2**20)


def gather_kernel(order, sides, bases, out, wide, values):
    points = sides.shape[0]
    wide[...] = sides[...].astype(f32)

    def body(step_no, carry):
        base = pl.multiple_of(step_no * unroll, unroll)
        for row in range(unroll):
            values[pl.ds(base + row, 1), :] = wide[pl.ds(order[0, base + row], 1), :]
        return carry

    lax.fori_loop(0, points // unroll, body, 0)
    projected = jnp.dot(bases[...], values[...].astype(bf16), preferred_element_type=f32)
    out[...] = projected.reshape(out.shape)


def gather_project(order, sides, flat_bases, levels):
    points, width = sides.shape
    return pl.pallas_call(
        gather_kernel,
        out_shape=jax.ShapeDtypeStruct((levels, flat_bases.shape[0] // levels, width), f32),
        in_specs=[smem, vmem, vmem],
        out_specs=vmem,
        scratch_shapes=[pltpu.VMEM((points, width), f32), pltpu.VMEM((points, width), f32)],
        compiler_params=params(24),
        cost_estimate=pl.CostEstimate(flops=7 * 10**9, bytes_accessed=5 * 10**6, transcendentals=0),
        name="gather_project",
    )(order, sides, flat_bases)


def split_three(wide):
    high = wide.astype(bf16).astype(f32)
    middle = (wide - high).astype(bf16).astype(f32)
    return high, middle, wide - high - middle


def prepare_kernel(own, coords, sides, couplings, row_features, column_features, sides_t, matrices):
    points = coords.shape[1]
    placed = (coords[...] - 0.5) * point_scale
    high, middle, low = split_three(placed)
    norm_parts = split_three(jnp.sum(placed * placed, axis=0, keepdims=True))
    ones = [jnp.ones((1, points), f32)] * 3
    filler = jnp.zeros((feature_rows - 24, points), f32)
    row_side = [-2 * high, -2 * high, -2 * middle, -2 * middle, -2 * high, -2 * low, *norm_parts, *ones, filler]
    column_side = [high, middle, high, middle, low, high, *ones, *norm_parts, filler]
    row_features[...] = jnp.concatenate(row_side, axis=0).T.astype(bf16)
    column_features[...] = jnp.concatenate(column_side, axis=0).astype(bf16)
    sides_t[...] = sides[...].astype(f32).T.astype(bf16)
    levels, rank, _ = matrices.shape
    nodes = couplings.shape[2]
    lane = lax.broadcasted_iota(jnp.int32, (8, nodes), 1)
    level = lax.broadcasted_iota(jnp.int32, (8, nodes), 0)
    leaf = own[0]
    chosen = jnp.zeros((8, nodes), f32)
    for level_no in range(levels):
        node = (nodes + 1 >> level_no + 1) + (leaf >> level_no + 1) - 1
        chosen = jnp.where((level == level_no) & (lane == node), 1.0, chosen)
    for row in range(rank):
        taken = lax.dot_general(
            chosen,
            couplings[row],
            (((1,), (1,)), ((), ())),
            precision=lax.Precision.HIGHEST,
            preferred_element_type=f32,
        )
        for level_no in range(levels):
            matrices[level_no, pl.ds(row, 1), :] = taken[level_no : level_no + 1, :]
    for level_no in range(levels):
        matrix = matrices[level_no]
        second = (leaf >> level_no & 1) == 1
        matrices[level_no] = jnp.where(second, matrix.T, matrix)


def prepare(own, coords, sides, couplings, levels):
    points, width = sides.shape
    rank = couplings.shape[0]
    return pl.pallas_call(
        prepare_kernel,
        out_shape=[
            jax.ShapeDtypeStruct((points, feature_rows), bf16),
            jax.ShapeDtypeStruct((feature_rows, points), bf16),
            jax.ShapeDtypeStruct((width, points), bf16),
            jax.ShapeDtypeStruct((levels, rank, rank), f32),
        ],
        in_specs=[smem, vmem, vmem, vmem],
        out_specs=[vmem] * 4,
        compiler_params=params(24),
        cost_estimate=pl.CostEstimate(flops=5 * 10**9, bytes_accessed=5 * 10**6, transcendentals=0),
        name="prepare",
    )(own, coords, sides, couplings)


def near_kernel(first, count, fresh, row_features, column_features, sides_t, *refs):
    before, total = refs if not fresh else (None, refs[0])
    points = column_features.shape[1]
    blocks = points // block
    half = blocks // 2
    total[...] = jnp.zeros_like(total) if fresh else before[...]
    for block_no in range(first, first + count):
        rows = pl.ds(block_no * block, block)
        others = [(block_no + step) % blocks for step in range(half + 1 if block_no < half else half)]
        runs = []
        for other in others:
            if len(runs) > 1 and runs[-1][0] + runs[-1][1] == other and runs[-1][1] < group_tiles:
                runs[-1][1] += 1
            else:
                runs.append([other, 1])
        own_sum = None
        for start, tiles in runs:
            columns = pl.ds(start * block, tiles * block)
            squared = jnp.dot(row_features[rows, :], column_features[:, columns], preferred_element_type=f32)
            squared = jnp.maximum(squared, 1e-30)
            scaled = squared * lax.rsqrt(squared)
            kernel = ((1.0 + log_two * scaled) * jnp.exp2(-scaled)).astype(bf16)
            part = lax.dot_general(
                sides_t[:, columns], kernel, (((1,), (1,)), ((), ())), preferred_element_type=f32
            )
            own_sum = part if own_sum is None else own_sum + part
            if start != block_no:
                total[:, columns] += jnp.dot(sides_t[:, rows], kernel, preferred_element_type=f32)
        total[:, rows] += own_sum


def near_part(first, count, features, before):
    width, points = features[2].shape
    entries = count * block * points // 2
    return pl.pallas_call(
        functools.partial(near_kernel, first, count, before is None),
        out_shape=jax.ShapeDtypeStruct((width, points), f32),
        in_specs=[vmem] * (3 if before is None else 4),
        out_specs=vmem,
        input_output_aliases={} if before is None else {3: 0},
        compiler_params=params(24),
        cost_estimate=pl.CostEstimate(
            flops=entries * 6 * width, bytes_accessed=6 * 10**6, transcendentals=2 * entries
        ),
        name="near_part",
    )(*features, *([] if before is None else [before]))


def tail_kernel(order, near_t, bases, matrices, *refs):
    siblings, (out, near, far) = refs[:-3], refs[-3:]
    points = near.shape[0]
    mixed = []
    for level_no, sibling in enumerate(siblings):
        factor_scale = 1.0 / math.sqrt(2**level_no * points)
        mixed.append(
            jnp.dot(
                matrices[level_no],
                sibling[0] * factor_scale,
                precision=lax.Precision.HIGHEST,
                preferred_element_type=f32,
            ).astype(bf16)
        )
    near[...] = kernel_amplitude * near_t[...].T
    far[...] = lax.dot_general(
        bases[...], jnp.concatenate(mixed, axis=0), (((0,), (0,)), ((), ())), preferred_element_type=f32
    )

    def body(step_no, carry):
        base = pl.multiple_of(step_no * unroll, unroll)
        for row in range(unroll):
            place = pl.ds(order[0, base + row], 1)
            out[place, :] = near[place, :] + far[pl.ds(base + row, 1), :]
        return carry

    lax.fori_loop(0, points // unroll, body, 0)


def tail(order, near_t, flat_bases, matrices, siblings):
    width, points = near_t.shape
    return pl.pallas_call(
        tail_kernel,
        out_shape=jax.ShapeDtypeStruct((points, width), f32),
        in_specs=[smem] + [vmem] * (3 + len(siblings)),
        out_specs=vmem,
        scratch_shapes=[pltpu.VMEM((points, width), f32), pltpu.VMEM((points, width), f32)],
        compiler_params=params(32),
        cost_estimate=pl.CostEstimate(flops=9 * 10**9, bytes_accessed=5 * 10**6, transcendentals=0),
        name="tail",
    )(order, near_t, flat_bases, matrices, *siblings)


def local(right_sides, coords, cluster_order, bases, coupling):
    levels, rank, points = bases.shape
    leaves = lax.axis_size("leaf")
    own = lax.axis_index("leaf").astype(jnp.int32).reshape(1)
    flat_bases = bases.reshape(levels * rank, points)
    held = gather_project(cluster_order, right_sides, flat_bases, levels)
    shares = iter(near_shares)
    near_t, first, siblings, features = None, 0, [], None
    for level_no, mask in enumerate(partner_masks):
        got = lax.ppermute(held, "leaf", [(leaf, leaf ^ mask) for leaf in range(leaves)])
        if level_no == 0:
            own, held = lax.optimization_barrier((own, held))
            *features, matrices = prepare(own, coords, right_sides, jnp.transpose(coupling, (1, 2, 0)), levels)
            got, matrices = lax.optimization_barrier((got, matrices))
        else:
            count = next(shares)
            features[1], held = lax.optimization_barrier((features[1], held))
            near_t = near_part(first, count, features, near_t)
            first += count
            got, near_t = lax.optimization_barrier((got, near_t))
        siblings.append(got[:1])
        held = held[1:] + got[1:]
    return tail(cluster_order, near_t, flat_bases, matrices, siblings)


def solution(mesh):
    in_specs = (P("leaf", None), P(None, "leaf"), P("leaf", None), P(None, None, "leaf"), P())
    out_specs = P("leaf", None)
    return jax.shard_map(local, mesh=mesh, in_specs=in_specs, out_specs=out_specs, check_vma=False)
```

```python
import functools
import math

import jax
import jax.numpy as jnp
from jax import lax
from jax.experimental import pallas as pl
from jax.experimental.pallas import tpu as pltpu
from jax.sharding import PartitionSpec as P

length_scale = 0.25
kernel_amplitude = 0.25
root_three = math.sqrt(3.0)
log_two = math.log(2.0)
point_scale = root_three / length_scale / log_two
block = 256
group_tiles = 2
feature_rows = 32
chunk = 512
near_shares = (7, 5, 4)
axis_steps = (2, 8, 32)

vmem = pl.BlockSpec(memory_space=pltpu.VMEM)
smem = pl.BlockSpec(memory_space=pltpu.SMEM)
hbm = pl.BlockSpec(memory_space=pltpu.HBM)
f32, bf16 = jnp.float32, jnp.bfloat16


def params(mib):
    return pltpu.CompilerParams(vmem_limit_bytes=mib * 2**20)


def gather_kernel(order, sides, bases, out, places, narrow, held, wide, even, odd, order_sem, side_sems, base_sems):
    points = sides.shape[0]
    quarter = points // 4
    rank = bases.shape[0] // base_sems.shape[0]
    copies = [pltpu.make_async_copy(order, places, order_sem)]
    for part in range(4):
        rows = pl.ds(part * quarter, quarter)
        copies.append(pltpu.make_async_copy(sides.at[rows, :], narrow.at[rows, :], side_sems.at[part]))
    base_copies = []
    for part in range(base_sems.shape[0]):
        rows = pl.ds(part * rank, rank)
        base_copies.append(pltpu.make_async_copy(bases.at[rows, :], held.at[rows, :], base_sems.at[part]))
    for copy in copies + base_copies:
        copy.start()
    for part, copy in enumerate(copies):
        copy.wait()
        if part:
            rows = pl.ds((part - 1) * quarter, quarter)
            wide[rows, :] = narrow[rows, :].astype(f32)

    def take(chunk_no, values):
        base = pl.multiple_of(chunk_no * chunk, chunk)
        for row in range(chunk):
            values[pl.ds(row, 1), :] = wide[pl.ds(places[0, base + row], 1), :]

    def project(chunk_no, values):
        columns = pl.ds(pl.multiple_of(chunk_no * chunk, chunk), chunk)
        return jnp.dot(held[:, columns], values[...].astype(bf16), preferred_element_type=f32)

    take(0, even)
    for copy in base_copies:
        copy.wait()
    out[...] = jnp.zeros_like(out)

    def body(pair_no, carry):
        first = 2 * pair_no
        out[...] += project(first, even).reshape(out.shape)
        take(first + 1, odd)
        out[...] += project(first + 1, odd).reshape(out.shape)
        take(first + 2, even)
        return carry

    pairs = points // chunk // 2
    lax.fori_loop(0, pairs - 1, body, 0)
    last = 2 * pairs - 2
    out[...] += project(last, even).reshape(out.shape)
    take(last + 1, odd)
    out[...] += project(last + 1, odd).reshape(out.shape)


def gather_project(order, sides, flat_bases, levels):
    points, width = sides.shape
    dma = pltpu.SemaphoreType.DMA
    return pl.pallas_call(
        gather_kernel,
        out_shape=jax.ShapeDtypeStruct((levels, flat_bases.shape[0] // levels, width), f32),
        in_specs=[hbm, hbm, hbm],
        out_specs=vmem,
        scratch_shapes=[
            pltpu.SMEM(order.shape, jnp.int32),
            pltpu.VMEM(sides.shape, bf16),
            pltpu.VMEM(flat_bases.shape, bf16),
            pltpu.VMEM((points, width), f32),
            pltpu.VMEM((chunk, width), f32),
            pltpu.VMEM((chunk, width), f32),
            dma,
            dma((4,)),
            dma((levels,)),
        ],
        compiler_params=params(58),
        cost_estimate=pl.CostEstimate(flops=7 * 10**9, bytes_accessed=5 * 10**6, transcendentals=0),
        name="gather_project",
    )(order, sides, flat_bases)


def split_three(wide):
    high = wide.astype(bf16).astype(f32)
    middle = (wide - high).astype(bf16).astype(f32)
    return high, middle, wide - high - middle


def prepare_kernel(own, coords_in, sides_in, couplings_in, *refs):
    row_features, column_features, sides_t, matrices, coords, sides, couplings, sems, coupling_sems = refs
    points = coords.shape[1]
    parts = coupling_sems.shape[0]
    share = couplings.shape[0] // parts
    copies = [
        pltpu.make_async_copy(coords_in, coords, sems.at[0]),
        pltpu.make_async_copy(sides_in, sides, sems.at[1]),
    ]
    for part in range(parts):
        rows = pl.ds(part * share, share)
        copies.append(pltpu.make_async_copy(couplings_in.at[rows], couplings.at[rows], coupling_sems.at[part]))
    for copy in copies:
        copy.start()
    copies[0].wait()
    placed = (coords[...] - 0.5) * point_scale
    high, middle, low = split_three(placed)
    norm_parts = split_three(jnp.sum(placed * placed, axis=0, keepdims=True))
    ones = [jnp.ones((1, points), f32)] * 3
    filler = jnp.zeros((feature_rows - 24, points), f32)
    row_side = [-2 * high, -2 * high, -2 * middle, -2 * middle, -2 * high, -2 * low, *norm_parts, *ones, filler]
    column_side = [high, middle, high, middle, low, high, *ones, *norm_parts, filler]
    row_features[...] = jnp.concatenate(row_side, axis=0).T.astype(bf16)
    column_features[...] = jnp.concatenate(column_side, axis=0).astype(bf16)
    copies[1].wait()
    sides_t[...] = sides[...].astype(f32).T.astype(bf16)
    levels, rank, _ = matrices.shape
    nodes = couplings.shape[2]
    lane = lax.broadcasted_iota(jnp.int32, (8, nodes), 1)
    level = lax.broadcasted_iota(jnp.int32, (8, nodes), 0)
    leaf = own[0]
    chosen = jnp.zeros((8, nodes), f32)
    for level_no in range(levels):
        node = (nodes + 1 >> level_no + 1) + (leaf >> level_no + 1) - 1
        chosen = jnp.where((level == level_no) & (lane == node), 1.0, chosen)
    chosen = chosen.astype(bf16)
    for copy in copies[2:]:
        copy.wait()
    for row in range(rank):
        taken = sum(
            lax.dot_general(
                chosen, part.astype(bf16), (((1,), (1,)), ((), ())), preferred_element_type=f32
            )
            for part in split_three(couplings[row])
        )
        for level_no in range(levels):
            matrices[level_no, pl.ds(row, 1), :] = taken[level_no : level_no + 1, :]
    for level_no in range(levels):
        matrix = matrices[level_no]
        second = (leaf >> level_no & 1) == 1
        matrices[level_no] = jnp.where(second, matrix.T, matrix)


def prepare(own, coords, sides, couplings, levels):
    points, width = sides.shape
    rank = couplings.shape[0]
    return pl.pallas_call(
        prepare_kernel,
        out_shape=[
            jax.ShapeDtypeStruct((points, feature_rows), bf16),
            jax.ShapeDtypeStruct((feature_rows, points), bf16),
            jax.ShapeDtypeStruct((width, points), bf16),
            jax.ShapeDtypeStruct((levels, rank, rank), f32),
        ],
        in_specs=[smem, hbm, hbm, hbm],
        out_specs=[vmem] * 4,
        scratch_shapes=[
            pltpu.VMEM(coords.shape, f32),
            pltpu.VMEM(sides.shape, bf16),
            pltpu.VMEM(couplings.shape, f32),
            pltpu.SemaphoreType.DMA((2,)),
            pltpu.SemaphoreType.DMA((4,)),
        ],
        compiler_params=params(44),
        cost_estimate=pl.CostEstimate(flops=5 * 10**9, bytes_accessed=5 * 10**6, transcendentals=0),
        name="prepare",
    )(own, coords, sides, couplings)


def mix(matrices, level_no, arrived, points):
    sibling = arrived[0][0]
    for other in arrived[1:]:
        sibling = sibling + other[0]
    factor_scale = 1.0 / math.sqrt(2**level_no * points)
    return jnp.dot(
        matrices[level_no], sibling * factor_scale, precision=lax.Precision.HIGHEST, preferred_element_type=f32
    ).astype(bf16)


def near_steps(first, count, blocks):
    half = blocks // 2
    steps = []
    for block_no in range(first, first + count):
        runs = [[block_no, 1]]
        for step in range(1, half + 1 if block_no < half else half):
            other = (block_no + step) % blocks
            if len(runs) > 1 and sum(runs[-1]) == other and runs[-1][1] < group_tiles:
                runs[-1][1] += 1
            else:
                runs.append([other, 1])
        steps += [(block_no, start, tiles) for start, tiles in runs]
    return steps


def near_blocks(first, count, row_features, column_features, sides_t, total, kernels):
    steps = near_steps(first, count, column_features.shape[1] // block)
    own = {}

    def entries(step_no):
        block_no, start, tiles = steps[step_no]
        columns = pl.ds(start * block, tiles * block)
        rows = pl.ds(block_no * block, block)
        squared = jnp.dot(row_features[rows, :], column_features[:, columns], preferred_element_type=f32)
        squared = jnp.maximum(squared, 1e-30)
        scaled = squared * lax.rsqrt(squared)
        kernel = (1.0 + log_two * scaled) * jnp.exp2(-scaled)
        kernels[step_no % 2, :, pl.ds(0, tiles * block)] = kernel.astype(bf16)

    def products(step_no):
        block_no, start, tiles = steps[step_no]
        columns = pl.ds(start * block, tiles * block)
        rows = pl.ds(block_no * block, block)
        kernel = kernels[step_no % 2, :, pl.ds(0, tiles * block)]
        part = lax.dot_general(
            sides_t[:, columns], kernel, (((1,), (1,)), ((), ())), preferred_element_type=f32
        )
        own[block_no] = own[block_no] + part if block_no in own else part
        if start != block_no:
            total[:, columns] += jnp.dot(sides_t[:, rows], kernel, preferred_element_type=f32)
        if step_no + 1 == len(steps) or steps[step_no + 1][0] != block_no:
            total[:, rows] += own.pop(block_no)

    for step_no in range(len(steps) + 1):
        if step_no < len(steps):
            entries(step_no)
        if step_no:
            products(step_no - 1)


def near_kernel(first, count, arrivals, fresh, row_features, column_features, sides_t, matrices, *refs):
    refs = list(refs)
    before = None if fresh else refs.pop(0)
    mixed, total, kernels = refs[-3:]
    points = column_features.shape[1]
    position = 0
    for slot, (level_no, number) in enumerate(arrivals):
        mixed[slot] = mix(matrices, level_no, refs[position : position + number], points)
        position += number
    total[...] = jnp.zeros_like(total) if fresh else before[...]
    near_blocks(first, count, row_features, column_features, sides_t, total, kernels)


def near_part(first, count, features, matrices, before, arrivals):
    width, points = features[2].shape
    rank = matrices.shape[1]
    entries = count * block * points // 2
    arrived = [array for _, arrays in arrivals for array in arrays]
    counts = tuple((level_no, len(arrays)) for level_no, arrays in arrivals)
    carried = [] if before is None else [before]
    return pl.pallas_call(
        functools.partial(near_kernel, first, count, counts, before is None),
        out_shape=[
            jax.ShapeDtypeStruct((len(arrivals), rank, width), bf16),
            jax.ShapeDtypeStruct((width, points), f32),
        ],
        in_specs=[vmem] * (4 + len(carried) + len(arrived)),
        out_specs=[vmem, vmem],
        scratch_shapes=[pltpu.VMEM((2, block, group_tiles * block), bf16)],
        input_output_aliases={} if before is None else {4: 1},
        compiler_params=params(16),
        cost_estimate=pl.CostEstimate(
            flops=entries * 6 * width, bytes_accessed=6 * 10**6, transcendentals=2 * entries
        ),
        name="near_part",
    )(*features, matrices, *carried, *arrived)


def tail_kernel(arrivals, order, near_t, bases, matrices, *refs):
    refs = list(refs)
    out, places, placed, even, odd, order_sem, out_sems = refs[-7:]
    points = near_t.shape[1]
    copy = pltpu.make_async_copy(order, places, order_sem)
    copy.start()
    arrived = refs[: sum(number for _, number in arrivals)]
    mixed = [earlier[slot] for earlier in refs[len(arrived) : -7] for slot in range(earlier.shape[0])]
    position = 0
    for level_no, number in arrivals:
        mixed.append(mix(matrices, level_no, arrived[position : position + number], points))
        position += number
    mixed_t = jnp.concatenate(mixed, axis=0).astype(f32).T.astype(bf16)
    copy.wait()

    def far(chunk_no, rows):
        columns = pl.ds(pl.multiple_of(chunk_no * chunk, chunk), chunk)
        rows[...] = jnp.dot(mixed_t, bases[:, columns], preferred_element_type=f32).T

    def scatter(chunk_no, rows):
        base = pl.multiple_of(chunk_no * chunk, chunk)
        for row in range(chunk):
            placed[pl.ds(places[0, base + row], 1), :] = rows[pl.ds(row, 1), :]

    far(0, even)

    def body(pair_no, carry):
        first = 2 * pair_no
        far(first + 1, odd)
        scatter(first, even)
        far(first + 2, even)
        scatter(first + 1, odd)
        return carry

    pairs = points // chunk // 2
    lax.fori_loop(0, pairs - 1, body, 0)
    last = 2 * pairs - 2
    far(last + 1, odd)
    scatter(last, even)
    scatter(last + 1, odd)
    copies = []
    for part in range(out_sems.shape[0]):
        rows = pl.ds(part * chunk, chunk)
        placed[rows, :] += kernel_amplitude * near_t[:, rows].T
        copies.append(pltpu.make_async_copy(placed.at[rows, :], out.at[rows, :], out_sems.at[part]))
        copies[-1].start()
    for copy in copies:
        copy.wait()


def tail(order, near_t, flat_bases, matrices, mixed, arrivals):
    width, points = near_t.shape
    arrived = [array for _, arrays in arrivals for array in arrays]
    counts = tuple((level_no, len(arrays)) for level_no, arrays in arrivals)
    dma = pltpu.SemaphoreType.DMA
    return pl.pallas_call(
        functools.partial(tail_kernel, counts),
        out_shape=jax.ShapeDtypeStruct((points, width), f32),
        in_specs=[hbm] + [vmem] * (3 + len(arrived) + len(mixed)),
        out_specs=hbm,
        scratch_shapes=[
            pltpu.SMEM(order.shape, jnp.int32),
            pltpu.VMEM((points, width), f32),
            pltpu.VMEM((chunk, width), f32),
            pltpu.VMEM((chunk, width), f32),
            dma,
            dma((points // chunk,)),
        ],
        compiler_params=params(16),
        cost_estimate=pl.CostEstimate(flops=9 * 10**9, bytes_accessed=5 * 10**6, transcendentals=0),
        name="tail",
    )(order, near_t, flat_bases, matrices, *arrived, *mixed)


def local(right_sides, coords, cluster_order, bases, coupling):
    levels, rank, points = bases.shape
    leaves = lax.axis_size("leaf")
    own = lax.axis_index("leaf").astype(jnp.int32).reshape(1)
    flat_bases = bases.reshape(levels * rank, points)

    def exchange(sent, mask):
        return lax.ppermute(sent, "leaf", [(leaf, leaf ^ mask) for leaf in range(leaves)])

    held = gather_project(cluster_order, right_sides, flat_bases, levels)
    got = exchange(held, 1)
    own, held = lax.optimization_barrier((own, held))
    *features, matrices = prepare(own, coords, right_sides, jnp.transpose(coupling, (1, 2, 0)), levels)
    got, matrices = lax.optimization_barrier((got, matrices))
    arrivals = [(0, [got])]
    held = held[1:] + got[1:]
    near_t, first, mixed = None, 0, []
    for axis_no, (step, count) in enumerate(zip(axis_steps, near_shares)):
        last = axis_no == len(axis_steps) - 1
        near_side = exchange(held[:1] if last else held, step)
        across = exchange(held[1:], 2 * step)
        corner = exchange(held[1:], 3 * step)
        features[1], held = lax.optimization_barrier((features[1], held))
        mixed_part, near_t = near_part(first, count, features, matrices, near_t, arrivals)
        mixed.append(mixed_part)
        first += count
        near_side, across, corner, near_t = lax.optimization_barrier((near_side, across, corner, near_t))
        arrivals = [(2 * axis_no + 1, [near_side]), (2 * axis_no + 2, [across, corner])]
        if not last:
            held = (held[2:] + near_side[2:]) + (across[1:] + corner[1:])
    return tail(cluster_order, near_t, flat_bases, matrices, mixed, arrivals)


def solution(mesh):
    in_specs = (P("leaf", None), P(None, "leaf"), P("leaf", None), P(None, None, "leaf"), P())
    out_specs = P("leaf", None)
    return jax.shard_map(local, mesh=mesh, in_specs=in_specs, out_specs=out_specs, check_vma=False)
```

```python
import functools
import math

import jax
import jax.numpy as jnp
from jax import lax
from jax.experimental import pallas as pl
from jax.experimental.pallas import tpu as pltpu
from jax.sharding import PartitionSpec as P

length_scale = 0.25
kernel_amplitude = 0.25
root_three = math.sqrt(3.0)
log_two = math.log(2.0)
point_scale = root_three / length_scale / log_two
block = 256
group_tiles = 2
feature_rows = 32
chunk = 512
near_shares = (2, 6, 4, 2)
axis_steps = (2, 8, 32)

vmem = pl.BlockSpec(memory_space=pltpu.VMEM)
smem = pl.BlockSpec(memory_space=pltpu.SMEM)
hbm = pl.BlockSpec(memory_space=pltpu.HBM)
f32, bf16 = jnp.float32, jnp.bfloat16


def params(mib):
    return pltpu.CompilerParams(vmem_limit_bytes=mib * 2**20)


def split_three(wide):
    high = wide.astype(bf16).astype(f32)
    middle = (wide - high).astype(bf16).astype(f32)
    return high, middle, wide - high - middle


def gather_kernel(own, order_in, sides_in, bases_in, coords_in, couplings_in, *refs):
    projected, row_features, column_features, sides_t, matrices = refs[:5]
    order, sides, bases, coords, couplings, wide = refs[5:11]
    first_sems, base_sems, coupling_sems = refs[11:14]
    values = refs[14:]
    points = sides.shape[0]
    levels, rank, _ = matrices.shape
    chunks = len(values)
    quarter = points // 4
    first_copies = [pltpu.make_async_copy(order_in, order, first_sems.at[0])]
    for part in range(4):
        rows = pl.ds(part * quarter, quarter)
        first_copies.append(pltpu.make_async_copy(sides_in.at[rows, :], sides.at[rows, :], first_sems.at[part + 1]))
    first_copies.append(pltpu.make_async_copy(coords_in, coords, first_sems.at[5]))
    coupling_copies, base_copies = [], []
    for part in range(4):
        rows = pl.ds(part * (rank // 4), rank // 4)
        coupling_copies.append(
            pltpu.make_async_copy(couplings_in.at[rows], couplings.at[rows], coupling_sems.at[part])
        )
    for part in range(levels):
        rows = pl.ds(part * rank, rank)
        base_copies.append(pltpu.make_async_copy(bases_in.at[rows, :], bases.at[rows, :], base_sems.at[part]))
    for copy in first_copies:
        copy.start()
    first_copies[0].wait()
    for part in range(4):
        first_copies[part + 1].wait()
        rows = pl.ds(part * quarter, quarter)
        wide[rows, :] = sides[rows, :].astype(f32)
    first_copies[5].wait()
    for copy in coupling_copies + base_copies:
        copy.start()

    nodes = couplings.shape[2]
    lane = lax.broadcasted_iota(jnp.int32, (8, nodes), 1)
    level = lax.broadcasted_iota(jnp.int32, (8, nodes), 0)
    leaf = own[0]
    chosen = jnp.zeros((8, nodes), f32)
    for level_no in range(levels):
        node = (nodes + 1 >> level_no + 1) + (leaf >> level_no + 1) - 1
        chosen = jnp.where((level == level_no) & (lane == node), 1.0, chosen)
    chosen = chosen.astype(bf16)

    def features(chunk_no):
        columns = pl.ds(chunk_no * chunk, chunk)
        placed = (coords[:, columns] - 0.5) * point_scale
        high, middle, low = split_three(placed)
        norm_parts = split_three(jnp.sum(placed * placed, axis=0, keepdims=True))
        ones = [jnp.ones((1, chunk), f32)] * 3
        filler = jnp.zeros((feature_rows - 24, chunk), f32)
        row_side = [-2 * high, -2 * high, -2 * middle, -2 * middle, -2 * high, -2 * low, *norm_parts, *ones, filler]
        column_side = [high, middle, high, middle, low, high, *ones, *norm_parts, filler]
        row_features[columns, :] = jnp.concatenate(row_side, axis=0).T.astype(bf16)
        column_features[:, columns] = jnp.concatenate(column_side, axis=0).astype(bf16)

    def transpose(chunk_no):
        columns = pl.ds(chunk_no * chunk, chunk)
        sides_t[:, columns] = wide[columns, :].T.astype(bf16)

    def select(row):
        taken = sum(
            lax.dot_general(chosen, part.astype(bf16), (((1,), (1,)), ((), ())), preferred_element_type=f32)
            for part in split_three(couplings[row])
        )
        for level_no in range(levels):
            matrices[level_no, pl.ds(row, 1), :] = taken[level_no : level_no + 1, :]

    def take(first, last):
        for row in range(first, last):
            place = pl.ds(row % chunk, 1)
            values[row // chunk][place, :] = wide[pl.ds(order[0, row], 1), :]

    def project(first, last):
        taken = jnp.concatenate([values[chunk_no][...].astype(bf16) for chunk_no in range(first, last)], axis=0)
        columns = pl.ds(first * chunk, (last - first) * chunk)
        part = jnp.dot(bases[:, columns], taken, preferred_element_type=f32).reshape(projected.shape)
        if first:
            projected[...] += part
        else:
            projected[...] = part

    beside = [[] for _ in range(chunks)]
    for chunk_no in range(chunks):
        beside[chunk_no] += [functools.partial(features, chunk_no), functools.partial(transpose, chunk_no)]
    late = chunks - 2
    for row in range(rank):
        beside[2 + row * late // rank].append(functools.partial(select, row))
    beside[4].append(functools.partial(project, 0, 2))
    beside[6].append(functools.partial(project, 2, 4))
    beside[7].append(functools.partial(project, 4, 6))
    for chunk_no in range(chunks):
        if chunk_no == 2:
            for copy in coupling_copies:
                copy.wait()
        if chunk_no == 4:
            for copy in base_copies:
                copy.wait()
        pieces = beside[chunk_no]
        for piece_no, piece in enumerate(pieces):
            first, last = (piece_no * chunk // len(pieces), (piece_no + 1) * chunk // len(pieces))
            take(chunk_no * chunk + first, chunk_no * chunk + last)
            piece()
    project(chunks - 2, chunks)
    for level_no in range(levels):
        matrix = matrices[level_no]
        second = (leaf >> level_no & 1) == 1
        matrices[level_no] = jnp.where(second, matrix.T, matrix)


def gather_project(own, order, sides, flat_bases, coords, couplings, levels):
    points, width = sides.shape
    rank = couplings.shape[0]
    dma = pltpu.SemaphoreType.DMA
    return pl.pallas_call(
        gather_kernel,
        out_shape=[
            pltpu.VMEM((levels, rank, width), f32),
            pltpu.VMEM((points, feature_rows), bf16),
            pltpu.VMEM((feature_rows, points), bf16),
            pltpu.VMEM((width, points), bf16),
            pltpu.VMEM((levels, rank, rank), f32),
        ],
        in_specs=[smem] + [hbm] * 5,
        out_specs=[vmem] * 5,
        scratch_shapes=[
            pltpu.SMEM(order.shape, jnp.int32),
            pltpu.VMEM(sides.shape, bf16),
            pltpu.VMEM(flat_bases.shape, bf16),
            pltpu.VMEM(coords.shape, f32),
            pltpu.VMEM(couplings.shape, f32),
            pltpu.VMEM((points, width), f32),
            dma((6,)),
            dma((levels,)),
            dma((4,)),
        ]
        + [pltpu.VMEM((chunk, width), f32)] * (points // chunk),
        compiler_params=params(32),
        cost_estimate=pl.CostEstimate(flops=7 * 10**9, bytes_accessed=5 * 10**6, transcendentals=0),
        name="gather_project",
    )(own, *(pltpu.with_memory_space_constraint(array, pltpu.HBM) for array in (order, sides, flat_bases, coords, couplings)))


def mix(matrices, level_no, arrived, points):
    sibling = arrived[0][0]
    for other in arrived[1:]:
        sibling = sibling + other[0]
    factor_scale = 1.0 / math.sqrt(2**level_no * points)
    return jnp.dot(
        matrices[level_no], sibling * factor_scale, precision=lax.Precision.HIGHEST, preferred_element_type=f32
    ).astype(bf16)


def near_steps(first, count, blocks):
    half = blocks // 2
    steps = []
    for block_no in range(first, first + count):
        runs = [[block_no, 1]]
        for step in range(1, half + 1 if block_no < half else half):
            other = (block_no + step) % blocks
            if len(runs) > 1 and sum(runs[-1]) == other and runs[-1][1] < group_tiles:
                runs[-1][1] += 1
            else:
                runs.append([other, 1])
        steps += [(block_no, start, tiles) for start, tiles in runs]
    return steps


def near_blocks(first, count, row_features, column_features, sides_t, total, kernels):
    steps = near_steps(first, count, column_features.shape[1] // block)
    own = {}

    def entries(step_no):
        block_no, start, tiles = steps[step_no]
        columns = pl.ds(start * block, tiles * block)
        rows = pl.ds(block_no * block, block)
        squared = jnp.dot(row_features[rows, :], column_features[:, columns], preferred_element_type=f32)
        squared = jnp.maximum(squared, 1e-30)
        scaled = squared * lax.rsqrt(squared)
        kernel = (1.0 + log_two * scaled) * jnp.exp2(-scaled)
        kernels[step_no % 2, :, pl.ds(0, tiles * block)] = kernel.astype(bf16)

    def products(step_no):
        block_no, start, tiles = steps[step_no]
        columns = pl.ds(start * block, tiles * block)
        rows = pl.ds(block_no * block, block)
        kernel = kernels[step_no % 2, :, pl.ds(0, tiles * block)]
        part = lax.dot_general(
            sides_t[:, columns], kernel, (((1,), (1,)), ((), ())), preferred_element_type=f32
        )
        own[block_no] = own[block_no] + part if block_no in own else part
        if start != block_no:
            total[:, columns] += jnp.dot(sides_t[:, rows], kernel, preferred_element_type=f32)
        if step_no + 1 == len(steps) or steps[step_no + 1][0] != block_no:
            total[:, rows] += own.pop(block_no)

    for step_no in range(len(steps) + 1):
        if step_no < len(steps):
            entries(step_no)
            yield
        if step_no:
            products(step_no - 1)
            yield


def near_kernel(first, count, arrivals, fresh, row_features, column_features, sides_t, matrices, *refs):
    refs = list(refs)
    before = None if fresh else refs.pop(0)
    total, kernels = refs[-2:]
    mixed = refs[-3] if arrivals else None
    points = column_features.shape[1]
    position = 0
    for slot, (level_no, number) in enumerate(arrivals):
        mixed[slot] = mix(matrices, level_no, refs[position : position + number], points)
        position += number
    total[...] = jnp.zeros_like(total) if fresh else before[...]
    for _ in near_blocks(first, count, row_features, column_features, sides_t, total, kernels):
        pass


def near_part(first, count, features, matrices, before, arrivals):
    width, points = features[2].shape
    rank = matrices.shape[1]
    entries = count * block * points // 2
    arrived = [array for _, arrays in arrivals for array in arrays]
    counts = tuple((level_no, len(arrays)) for level_no, arrays in arrivals)
    carried = [] if before is None else [before]
    mixed_shape = [jax.ShapeDtypeStruct((len(arrivals), rank, width), bf16)] if arrivals else []
    return pl.pallas_call(
        functools.partial(near_kernel, first, count, counts, before is None),
        out_shape=mixed_shape + [jax.ShapeDtypeStruct((width, points), f32)],
        in_specs=[vmem] * (4 + len(carried) + len(arrived)),
        out_specs=[vmem] * (len(mixed_shape) + 1),
        scratch_shapes=[pltpu.VMEM((2, block, group_tiles * block), bf16)],
        input_output_aliases={} if before is None else {4: len(mixed_shape)},
        compiler_params=params(16),
        cost_estimate=pl.CostEstimate(
            flops=entries * 6 * width, bytes_accessed=6 * 10**6, transcendentals=2 * entries
        ),
        name="near_part",
    )(*features, matrices, *carried, *arrived)


def tail_kernel(arrivals, first, order_in, before, bases, matrices, row_features, column_features, sides_t, *refs):
    refs = list(refs)
    out, order, total, kernels, placed, order_sem, out_sems, *far_rows = refs[-(7 + before.shape[1] // chunk) :]
    refs = refs[: -(7 + len(far_rows))]
    points = before.shape[1]
    copy = pltpu.make_async_copy(order_in, order, order_sem)
    copy.start()
    arrived = refs[: sum(number for _, number in arrivals)]
    mixed = [earlier[slot] for earlier in refs[len(arrived) :] for slot in range(earlier.shape[0])]
    position = 0
    for level_no, number in arrivals:
        mixed.append(mix(matrices, level_no, arrived[position : position + number], points))
        position += number
    mixed_t = jnp.concatenate(mixed, axis=0).astype(f32).T.astype(bf16)
    copy.wait()

    def far(chunk_no):
        columns = pl.ds(chunk_no * chunk, chunk)
        far_rows[chunk_no][...] = jnp.dot(mixed_t, bases[:, columns], preferred_element_type=f32).T

    def scatter(first_row, last_row):
        for row in range(first_row, last_row):
            value = far_rows[row // chunk][pl.ds(row % chunk, 1), :]
            placed[pl.ds(order[0, row], 1), :] = value

    total[...] = before[...]
    blocks = points // block
    near = near_blocks(first, blocks - first, row_features, column_features, sides_t, total, kernels)
    far(0)
    share = chunk // 4
    for row in range(0, points, share):
        if row % chunk == 0 and row + chunk < points:
            far(row // chunk + 1)
        scatter(row, row + share)
        next(near, None)
    for _ in near:
        pass
    copies = []
    for part in range(out_sems.shape[0]):
        rows = pl.ds(part * chunk, chunk)
        placed[rows, :] += kernel_amplitude * total[:, rows].T
        copies.append(pltpu.make_async_copy(placed.at[rows, :], out.at[rows, :], out_sems.at[part]))
        copies[-1].start()
    for copy in copies:
        copy.wait()


def tail(order, near_t, flat_bases, matrices, features, first, mixed, arrivals):
    width, points = near_t.shape
    arrived = [array for _, arrays in arrivals for array in arrays]
    counts = tuple((level_no, len(arrays)) for level_no, arrays in arrivals)
    dma = pltpu.SemaphoreType.DMA
    return pl.pallas_call(
        functools.partial(tail_kernel, counts, first),
        out_shape=jax.ShapeDtypeStruct((points, width), f32),
        in_specs=[hbm] + [vmem] * (6 + len(arrived) + len(mixed)),
        out_specs=hbm,
        scratch_shapes=[
            pltpu.SMEM(order.shape, jnp.int32),
            pltpu.VMEM((width, points), f32),
            pltpu.VMEM((2, block, group_tiles * block), bf16),
            pltpu.VMEM((points, width), f32),
            dma,
            dma((points // chunk,)),
        ]
        + [pltpu.VMEM((chunk, width), f32)] * (points // chunk),
        compiler_params=params(20),
        cost_estimate=pl.CostEstimate(flops=9 * 10**9, bytes_accessed=5 * 10**6, transcendentals=0),
        name="tail",
    )(order, near_t, flat_bases, matrices, *features, *arrived, *mixed)


def local(right_sides, coords, cluster_order, bases, coupling):
    levels, rank, points = bases.shape
    leaves = lax.axis_size("leaf")
    own = lax.axis_index("leaf").astype(jnp.int32).reshape(1)
    flat_bases = bases.reshape(levels * rank, points)

    def exchange(sent, mask):
        return lax.ppermute(sent, "leaf", [(leaf, leaf ^ mask) for leaf in range(leaves)])

    couplings = jnp.transpose(coupling, (1, 2, 0))
    held, *features, matrices = gather_project(
        own, cluster_order, right_sides, flat_bases, coords, couplings, levels
    )
    got = exchange(held, 1)
    near_t = near_part(0, near_shares[0], features, matrices, None, [])[-1]
    got, near_t = lax.optimization_barrier((got, near_t))
    arrivals = [(0, [got])]
    held = held[1:] + got[1:]
    first, mixed = near_shares[0], []
    for axis_no, (step, count) in enumerate(zip(axis_steps, near_shares[1:])):
        last = axis_no == len(axis_steps) - 1
        near_side = exchange(held[:1] if last else held, step)
        across = exchange(held[1:], 2 * step)
        corner = exchange(held[1:], 3 * step)
        features[1], held = lax.optimization_barrier((features[1], held))
        mixed_part, near_t = near_part(first, count, features, matrices, near_t, arrivals)
        mixed.append(mixed_part)
        first += count
        near_side, across, corner, near_t = lax.optimization_barrier((near_side, across, corner, near_t))
        arrivals = [(2 * axis_no + 1, [near_side]), (2 * axis_no + 2, [across, corner])]
        if not last:
            held = (held[2:] + near_side[2:]) + (across[1:] + corner[1:])
    return tail(cluster_order, near_t, flat_bases, matrices, features, first, mixed, arrivals)


def solution(mesh):
    in_specs = (P("leaf", None), P(None, "leaf"), P("leaf", None), P(None, None, "leaf"), P())
    out_specs = P("leaf", None)
    return jax.shard_map(local, mesh=mesh, in_specs=in_specs, out_specs=out_specs, check_vma=False)
```

```python
import functools
import math

import jax
import jax.numpy as jnp
from jax import lax
from jax.experimental import pallas as pl
from jax.experimental.pallas import tpu as pltpu
from jax.sharding import PartitionSpec as P

length_scale = 0.25
kernel_amplitude = 0.25
root_three = math.sqrt(3.0)
log_two = math.log(2.0)
point_scale = root_three / length_scale / log_two
block = 256
group_tiles = 2
feature_rows = 32
chunk = 512
near_shares = (2, 3, 2, 2, 2, 2, 1)
axis_steps = (2, 8, 32)

vmem = pl.BlockSpec(memory_space=pltpu.VMEM)
smem = pl.BlockSpec(memory_space=pltpu.SMEM)
hbm = pl.BlockSpec(memory_space=pltpu.HBM)
f32, bf16 = jnp.float32, jnp.bfloat16


def params(mib):
    return pltpu.CompilerParams(vmem_limit_bytes=mib * 2**20)


def split_three(wide):
    high = wide.astype(bf16).astype(f32)
    middle = (wide - high).astype(bf16).astype(f32)
    return high, middle, wide - high - middle


def gather_kernel(own, order_in, sides_in, bases_in, coords_in, couplings_in, *refs):
    projected, row_features, column_features, sides_t, matrices = refs[:5]
    order, sides, bases, coords, couplings, wide = refs[5:11]
    first_sems, base_sems, coupling_sems = refs[11:14]
    values = refs[14:]
    points = sides.shape[0]
    levels, rank, _ = matrices.shape
    chunks = len(values)
    quarter = points // 4
    first_copies = [pltpu.make_async_copy(order_in, order, first_sems.at[0])]
    for part in range(4):
        rows = pl.ds(part * quarter, quarter)
        first_copies.append(pltpu.make_async_copy(sides_in.at[rows, :], sides.at[rows, :], first_sems.at[part + 1]))
    first_copies.append(pltpu.make_async_copy(coords_in, coords, first_sems.at[5]))
    coupling_copies, base_copies = [], []
    for part in range(4):
        rows = pl.ds(part * (rank // 4), rank // 4)
        coupling_copies.append(
            pltpu.make_async_copy(couplings_in.at[rows], couplings.at[rows], coupling_sems.at[part])
        )
    for part in range(levels):
        rows = pl.ds(part * rank, rank)
        base_copies.append(pltpu.make_async_copy(bases_in.at[rows, :], bases.at[rows, :], base_sems.at[part]))
    for copy in first_copies:
        copy.start()
    first_copies[0].wait()
    for part in range(4):
        first_copies[part + 1].wait()
        rows = pl.ds(part * quarter, quarter)
        wide[rows, :] = sides[rows, :].astype(f32)
    first_copies[5].wait()
    for copy in coupling_copies + base_copies:
        copy.start()

    nodes = couplings.shape[2]
    lane = lax.broadcasted_iota(jnp.int32, (8, nodes), 1)
    level = lax.broadcasted_iota(jnp.int32, (8, nodes), 0)
    leaf = own[0]
    chosen = jnp.zeros((8, nodes), f32)
    for level_no in range(levels):
        node = (nodes + 1 >> level_no + 1) + (leaf >> level_no + 1) - 1
        chosen = jnp.where((level == level_no) & (lane == node), 1.0, chosen)
    chosen = chosen.astype(bf16)

    def features(chunk_no):
        columns = pl.ds(chunk_no * chunk, chunk)
        placed = (coords[:, columns] - 0.5) * point_scale
        high, middle, low = split_three(placed)
        norm_parts = split_three(jnp.sum(placed * placed, axis=0, keepdims=True))
        ones = [jnp.ones((1, chunk), f32)] * 3
        filler = jnp.zeros((feature_rows - 24, chunk), f32)
        row_side = [-2 * high, -2 * high, -2 * middle, -2 * middle, -2 * high, -2 * low, *norm_parts, *ones, filler]
        column_side = [high, middle, high, middle, low, high, *ones, *norm_parts, filler]
        row_features[columns, :] = jnp.concatenate(row_side, axis=0).T.astype(bf16)
        column_features[:, columns] = jnp.concatenate(column_side, axis=0).astype(bf16)

    def transpose(chunk_no):
        columns = pl.ds(chunk_no * chunk, chunk)
        sides_t[:, columns] = wide[columns, :].T.astype(bf16)

    def select(row):
        taken = sum(
            lax.dot_general(chosen, part.astype(bf16), (((1,), (1,)), ((), ())), preferred_element_type=f32)
            for part in split_three(couplings[row])
        )
        for level_no in range(levels):
            matrices[level_no, pl.ds(row, 1), :] = taken[level_no : level_no + 1, :]

    def take(first, last):
        for row in range(first, last):
            place = pl.ds(row % chunk, 1)
            values[row // chunk][place, :] = wide[pl.ds(order[0, row], 1), :]

    def project(first, last):
        taken = jnp.concatenate([values[chunk_no][...].astype(bf16) for chunk_no in range(first, last)], axis=0)
        columns = pl.ds(first * chunk, (last - first) * chunk)
        part = jnp.dot(bases[:, columns], taken, preferred_element_type=f32).reshape(projected.shape)
        if first:
            projected[...] += part
        else:
            projected[...] = part

    beside = [[] for _ in range(chunks)]
    for chunk_no in range(chunks):
        beside[chunk_no] += [functools.partial(features, chunk_no), functools.partial(transpose, chunk_no)]
    late = chunks - 2
    for row in range(rank):
        beside[2 + row * late // rank].append(functools.partial(select, row))
    beside[4].append(functools.partial(project, 0, 2))
    beside[6].append(functools.partial(project, 2, 4))
    beside[7].append(functools.partial(project, 4, 6))
    for chunk_no in range(chunks):
        if chunk_no == 2:
            for copy in coupling_copies:
                copy.wait()
        if chunk_no == 4:
            for copy in base_copies:
                copy.wait()
        pieces = beside[chunk_no]
        for piece_no, piece in enumerate(pieces):
            first, last = (piece_no * chunk // len(pieces), (piece_no + 1) * chunk // len(pieces))
            take(chunk_no * chunk + first, chunk_no * chunk + last)
            piece()
    project(chunks - 2, chunks)
    for level_no in range(levels):
        matrix = matrices[level_no]
        second = (leaf >> level_no & 1) == 1
        matrices[level_no] = jnp.where(second, matrix.T, matrix)


def gather_project(own, order, sides, flat_bases, coords, couplings, levels):
    points, width = sides.shape
    rank = couplings.shape[0]
    dma = pltpu.SemaphoreType.DMA
    return pl.pallas_call(
        gather_kernel,
        out_shape=[
            pltpu.VMEM((levels, rank, width), f32),
            pltpu.VMEM((points, feature_rows), bf16),
            pltpu.VMEM((feature_rows, points), bf16),
            pltpu.VMEM((width, points), bf16),
            pltpu.VMEM((levels, rank, rank), f32),
        ],
        in_specs=[smem] + [hbm] * 5,
        out_specs=[vmem] * 5,
        scratch_shapes=[
            pltpu.SMEM(order.shape, jnp.int32),
            pltpu.VMEM(sides.shape, bf16),
            pltpu.VMEM(flat_bases.shape, bf16),
            pltpu.VMEM(coords.shape, f32),
            pltpu.VMEM(couplings.shape, f32),
            pltpu.VMEM((points, width), f32),
            dma((6,)),
            dma((levels,)),
            dma((4,)),
        ]
        + [pltpu.VMEM((chunk, width), f32)] * (points // chunk),
        compiler_params=params(32),
        cost_estimate=pl.CostEstimate(flops=7 * 10**9, bytes_accessed=5 * 10**6, transcendentals=0),
        name="gather_project",
    )(own, *(pltpu.with_memory_space_constraint(array, pltpu.HBM) for array in (order, sides, flat_bases, coords, couplings)))


def mix(matrices, level_no, sibling, points):
    factor_scale = 1.0 / math.sqrt(2**level_no * points)
    return jnp.dot(
        matrices[level_no], sibling * factor_scale, precision=lax.Precision.HIGHEST, preferred_element_type=f32
    ).astype(bf16)


def near_steps(first, count, blocks):
    half = blocks // 2
    steps = []
    for block_no in range(first, first + count):
        runs = [[block_no, 1]]
        for step in range(1, half + 1 if block_no < half else half):
            other = (block_no + step) % blocks
            if len(runs) > 1 and sum(runs[-1]) == other and runs[-1][1] < group_tiles:
                runs[-1][1] += 1
            else:
                runs.append([other, 1])
        steps += [(block_no, start, tiles) for start, tiles in runs]
    return steps


def near_blocks(first, count, row_features, column_features, sides_t, total, kernels):
    steps = near_steps(first, count, column_features.shape[1] // block)
    own = {}

    def entries(step_no):
        block_no, start, tiles = steps[step_no]
        columns = pl.ds(start * block, tiles * block)
        rows = pl.ds(block_no * block, block)
        squared = jnp.dot(row_features[rows, :], column_features[:, columns], preferred_element_type=f32)
        squared = jnp.maximum(squared, 1e-30)
        scaled = squared * lax.rsqrt(squared)
        kernel = (1.0 + log_two * scaled) * jnp.exp2(-scaled)
        kernels[step_no % 2, :, pl.ds(0, tiles * block)] = kernel.astype(bf16)

    def products(step_no):
        block_no, start, tiles = steps[step_no]
        columns = pl.ds(start * block, tiles * block)
        rows = pl.ds(block_no * block, block)
        kernel = kernels[step_no % 2, :, pl.ds(0, tiles * block)]
        part = lax.dot_general(
            sides_t[:, columns], kernel, (((1,), (1,)), ((), ())), preferred_element_type=f32
        )
        own[block_no] = own[block_no] + part if block_no in own else part
        if start != block_no:
            total[:, columns] += jnp.dot(sides_t[:, rows], kernel, preferred_element_type=f32)
        if step_no + 1 == len(steps) or steps[step_no + 1][0] != block_no:
            total[:, rows] += own.pop(block_no)

    for step_no in range(len(steps) + 1):
        if step_no < len(steps):
            entries(step_no)
            yield
        if step_no:
            products(step_no - 1)
            yield


def near_kernel(first, count, arrivals, fresh, row_features, column_features, sides_t, matrices, *refs):
    refs = list(refs)
    before = None if fresh else refs.pop(0)
    total, kernels = refs[-2:]
    mixed = refs[-3] if arrivals else None
    points = column_features.shape[1]
    for slot, level_no in enumerate(arrivals):
        mixed[slot] = mix(matrices, level_no, refs[0][slot], points)
    if fresh:
        total[...] = jnp.zeros_like(total)
    else:
        total[...] = before[...]
    for _ in near_blocks(first, count, row_features, column_features, sides_t, total, kernels):
        pass


def near_part(first, count, features, matrices, before, arrivals=(), sums=None):
    width, points = features[2].shape
    rank = matrices.shape[1]
    entries = count * block * points // 2
    arrived = [sums for sums in [sums] if arrivals]
    carried = [] if before is None else [before]
    mixed_shape = [jax.ShapeDtypeStruct((len(arrivals), rank, width), bf16)] if arrivals else []
    return pl.pallas_call(
        functools.partial(near_kernel, first, count, arrivals, before is None),
        out_shape=mixed_shape + [jax.ShapeDtypeStruct((width, points), f32)],
        in_specs=[vmem] * (4 + len(carried) + len(arrived)),
        out_specs=[vmem] * (len(mixed_shape) + 1),
        scratch_shapes=[pltpu.VMEM((2, block, group_tiles * block), bf16)],
        input_output_aliases={} if before is None else {4: len(mixed_shape)},
        compiler_params=params(16),
        cost_estimate=pl.CostEstimate(
            flops=entries * 6 * width, bytes_accessed=6 * 10**6, transcendentals=2 * entries
        ),
        name="near_part",
    )(*features, matrices, *carried, *arrived)


def tail_kernel(arrivals, first, order_in, before, bases, matrices, row_features, column_features, sides_t, *refs):
    refs = list(refs)
    out, order, total, kernels, placed, order_sem, out_sems, *far_rows = refs[-(7 + before.shape[1] // chunk) :]
    refs = refs[: -(7 + len(far_rows))]
    points = before.shape[1]
    copy = pltpu.make_async_copy(order_in, order, order_sem)
    copy.start()
    mixed = [earlier[slot] for earlier in refs[1:] for slot in range(earlier.shape[0])]
    mixed += [mix(matrices, level_no, refs[0][slot], points) for slot, level_no in enumerate(arrivals)]
    mixed_t = jnp.concatenate(mixed, axis=0).astype(f32).T.astype(bf16)
    copy.wait()

    def far(chunk_no):
        columns = pl.ds(chunk_no * chunk, chunk)
        far_rows[chunk_no][...] = jnp.dot(mixed_t, bases[:, columns], preferred_element_type=f32).T

    def scatter(first_row, last_row):
        for row in range(first_row, last_row):
            value = far_rows[row // chunk][pl.ds(row % chunk, 1), :]
            placed[pl.ds(order[0, row], 1), :] = value

    total[...] = before[...]
    blocks = points // block
    near = near_blocks(first, blocks - first, row_features, column_features, sides_t, total, kernels)
    far(0)
    share = chunk // 4
    for row in range(0, points, share):
        if row % chunk == 0 and row + chunk < points:
            far(row // chunk + 1)
        scatter(row, row + share)
        next(near, None)
    for _ in near:
        pass
    copies = []
    for part in range(out_sems.shape[0]):
        rows = pl.ds(part * chunk, chunk)
        placed[rows, :] += kernel_amplitude * total[:, rows].T
        copies.append(pltpu.make_async_copy(placed.at[rows, :], out.at[rows, :], out_sems.at[part]))
        copies[-1].start()
    for copy in copies:
        copy.wait()


def tail(order, near_t, flat_bases, matrices, features, first, mixed, arrivals, sums):
    width, points = near_t.shape
    dma = pltpu.SemaphoreType.DMA
    return pl.pallas_call(
        functools.partial(tail_kernel, arrivals, first),
        out_shape=jax.ShapeDtypeStruct((points, width), f32),
        in_specs=[hbm] + [vmem] * (7 + len(mixed)),
        out_specs=hbm,
        scratch_shapes=[
            pltpu.SMEM(order.shape, jnp.int32),
            pltpu.VMEM((width, points), f32),
            pltpu.VMEM((2, block, group_tiles * block), bf16),
            pltpu.VMEM((points, width), f32),
            dma,
            dma((points // chunk,)),
        ]
        + [pltpu.VMEM((chunk, width), f32)] * (points // chunk),
        compiler_params=params(20),
        cost_estimate=pl.CostEstimate(flops=9 * 10**9, bytes_accessed=5 * 10**6, transcendentals=0),
        name="tail",
    )(order, near_t, flat_bases, matrices, *features, sums, *mixed)


def local(right_sides, coords, cluster_order, bases, coupling):
    levels, rank, points = bases.shape
    leaves = lax.axis_size("leaf")
    leaf = lax.axis_index("leaf").astype(jnp.int32)
    core = leaf & 1
    half = rank // 2
    flat_bases = bases.reshape(levels * rank, points)
    couplings = jnp.transpose(coupling, (1, 2, 0))
    held, *features, matrices = gather_project(
        leaf.reshape(1), cluster_order, right_sides, flat_bases, coords, couplings, levels
    )
    shares = iter(near_shares)
    near_t, first, mixed = None, 0, []

    def exchange(sent, even_mask, odd_mask):
        pairs = [(source, source ^ (odd_mask if source & 1 else even_mask)) for source in range(leaves)]
        return lax.ppermute(sent, "leaf", pairs)

    def beside(held, received, arrivals=(), sums=None):
        nonlocal near_t, first
        count = next(shares)
        features[1], held = lax.optimization_barrier((features[1], held))
        *mixed_part, near_t = near_part(first, count, features, matrices, near_t, arrivals, sums)
        mixed.extend(mixed_part)
        first += count
        *received, near_t = lax.optimization_barrier((*received, near_t))
        return received

    (got,) = beside(held, [exchange(held, 1, 1)])
    arrivals, sums = (0,), got
    held = held[1:] + got[1:]
    own_half = (lax.broadcasted_iota(jnp.int32, (1, rank, 1), 1) // half == core).astype(f32)
    for axis_no, step in enumerate(axis_steps):
        one_side = jnp.concatenate([jnp.where(core == 0, held[:1], held[1:2]), held[2:]], axis=0)
        across = lax.dynamic_slice_in_dim(held[1:], core * half, half, 1)
        received = [exchange(one_side, step, 3 * step), exchange(across, 2 * step, 2 * step)]
        one_side, across = beside(one_side, received, arrivals, sums)
        across = jnp.concatenate([across, across], axis=1) * own_half
        lower = jnp.where(core == 0, one_side[:1], 0.0)
        upper = jnp.where(core == 0, 0.0, one_side[:1]) + across[:1]
        part = jnp.concatenate([lower, upper, one_side[1:] + across[1:]], axis=0)
        (other,) = beside(part, [exchange(part, 1, 1)])
        sums = part + other
        arrivals = (2 * axis_no + 1, 2 * axis_no + 2)
        held = held[2:] + sums[2:]
    return tail(cluster_order, near_t, flat_bases, matrices, features, first, mixed, arrivals, sums)


def solution(mesh):
    in_specs = (P("leaf", None), P(None, "leaf"), P("leaf", None), P(None, None, "leaf"), P())
    out_specs = P("leaf", None)
    return jax.shard_map(local, mesh=mesh, in_specs=in_specs, out_specs=out_specs, check_vma=False)
```

```python
import functools
import math

import jax
import jax.numpy as jnp
from jax import lax
from jax.experimental import pallas as pl
from jax.experimental.pallas import tpu as pltpu
from jax.sharding import PartitionSpec as P

length_scale = 0.25
kernel_amplitude = 0.25
root_three = math.sqrt(3.0)
log_two = math.log(2.0)
point_scale = root_three / length_scale / log_two
block = 256
group_tiles = 2
feature_rows = 32
chunk = 512
near_shares = (6, 5, 3)
axis_steps = (2, 8, 32)

vmem = pl.BlockSpec(memory_space=pltpu.VMEM)
smem = pl.BlockSpec(memory_space=pltpu.SMEM)
hbm = pl.BlockSpec(memory_space=pltpu.HBM)
f32, bf16 = jnp.float32, jnp.bfloat16


def params(mib):
    return pltpu.CompilerParams(vmem_limit_bytes=mib * 2**20)


def split_three(wide):
    high = wide.astype(bf16).astype(f32)
    middle = (wide - high).astype(bf16).astype(f32)
    return high, middle, wide - high - middle


def gather_kernel(order_in, sides_in, bases_in, coords_in, couplings_in, *refs):
    projected, sides, coords, couplings, order, bases, wide, first_sems, base_sems, other_sems, *values = refs
    points = sides.shape[0]
    levels = projected.shape[0]
    chunks = len(values)
    quarter = points // 4
    first_copies = [pltpu.make_async_copy(order_in, order, first_sems.at[0])]
    for part in range(4):
        rows = pl.ds(part * quarter, quarter)
        first_copies.append(pltpu.make_async_copy(sides_in.at[rows, :], sides.at[rows, :], first_sems.at[part + 1]))
    rank = bases.shape[0] // levels
    base_copies = []
    for part in range(levels):
        rows = pl.ds(part * rank, rank)
        base_copies.append(pltpu.make_async_copy(bases_in.at[rows, :], bases.at[rows, :], base_sems.at[part]))
    other_copies = [
        pltpu.make_async_copy(coords_in, coords, other_sems.at[0]),
        pltpu.make_async_copy(couplings_in, couplings, other_sems.at[1]),
    ]
    for copy in first_copies:
        copy.start()
    for part, copy in enumerate(first_copies):
        copy.wait()
        if part:
            rows = pl.ds((part - 1) * quarter, quarter)
            wide[rows, :] = sides[rows, :].astype(f32)
    for copy in base_copies + other_copies:
        copy.start()

    def take(chunk_no):
        for row in range(chunk):
            place = order[0, chunk_no * chunk + row]
            values[chunk_no][pl.ds(row, 1), :] = wide[pl.ds(place, 1), :]

    def project(first, last):
        taken = jnp.concatenate([values[chunk_no][...].astype(bf16) for chunk_no in range(first, last)], axis=0)
        columns = pl.ds(first * chunk, (last - first) * chunk)
        part = jnp.dot(bases[:, columns], taken, preferred_element_type=f32).reshape(projected.shape)
        if first:
            projected[...] += part
        else:
            projected[...] = part

    for chunk_no in range(chunks):
        if chunk_no == chunks - 3:
            for copy in base_copies:
                copy.wait()
            project(0, chunks - 4)
        if chunk_no == chunks - 1:
            project(chunks - 4, chunks - 2)
        take(chunk_no)
    project(chunks - 2, chunks)
    for copy in other_copies:
        copy.wait()


def gather_project(order, sides, flat_bases, coords, couplings, levels):
    points, width = sides.shape
    dma = pltpu.SemaphoreType.DMA
    inputs = (order, sides, flat_bases, coords, couplings)
    return pl.pallas_call(
        gather_kernel,
        out_shape=[
            pltpu.VMEM((levels, flat_bases.shape[0] // levels, width), f32),
            pltpu.VMEM(sides.shape, bf16),
            pltpu.VMEM(coords.shape, f32),
            pltpu.VMEM(couplings.shape, f32),
        ],
        in_specs=[hbm] * 5,
        out_specs=[vmem] * 4,
        scratch_shapes=[
            pltpu.SMEM(order.shape, jnp.int32),
            pltpu.VMEM(flat_bases.shape, bf16),
            pltpu.VMEM((points, width), f32),
            dma((5,)),
            dma((levels,)),
            dma((2,)),
        ]
        + [pltpu.VMEM((chunk, width), f32)] * (points // chunk),
        compiler_params=params(32),
        cost_estimate=pl.CostEstimate(flops=7 * 10**9, bytes_accessed=5 * 10**6, transcendentals=0),
        name="gather_project",
    )(*(pltpu.with_memory_space_constraint(array, pltpu.HBM) for array in inputs))


def prepare_kernel(coords, sides, row_features, column_features, sides_t):
    points = coords.shape[1]
    placed = (coords[...] - 0.5) * point_scale
    high, middle, low = split_three(placed)
    norm_parts = split_three(jnp.sum(placed * placed, axis=0, keepdims=True))
    ones = [jnp.ones((1, points), f32)] * 3
    filler = jnp.zeros((feature_rows - 24, points), f32)
    row_side = [-2 * high, -2 * high, -2 * middle, -2 * middle, -2 * high, -2 * low, *norm_parts, *ones, filler]
    column_side = [high, middle, high, middle, low, high, *ones, *norm_parts, filler]
    row_features[...] = jnp.concatenate(row_side, axis=0).T.astype(bf16)
    column_features[...] = jnp.concatenate(column_side, axis=0).astype(bf16)
    sides_t[...] = sides[...].astype(f32).T.astype(bf16)


def prepare(coords, sides):
    points, width = sides.shape
    return pl.pallas_call(
        prepare_kernel,
        out_shape=[
            pltpu.VMEM((points, feature_rows), bf16),
            pltpu.VMEM((feature_rows, points), bf16),
            pltpu.VMEM((width, points), bf16),
        ],
        in_specs=[vmem] * 2,
        out_specs=[vmem] * 3,
        compiler_params=params(16),
        cost_estimate=pl.CostEstimate(flops=3 * 10**9, bytes_accessed=3 * 10**6, transcendentals=0),
        name="prepare",
    )(coords, sides)


def mix(matrices, level_no, arrived, points):
    sibling = arrived[0][0]
    for other in arrived[1:]:
        sibling = sibling + other[0]
    factor_scale = 1.0 / math.sqrt(2**level_no * points)
    return jnp.dot(
        matrices[level_no], sibling * factor_scale, precision=lax.Precision.HIGHEST, preferred_element_type=f32
    ).astype(bf16)


def near_steps(first, count, blocks):
    half = blocks // 2
    steps = []
    for block_no in range(first, first + count):
        runs = [[block_no, 1]]
        for step in range(1, half + 1 if block_no < half else half):
            other = (block_no + step) % blocks
            if len(runs) > 1 and sum(runs[-1]) == other and runs[-1][1] < group_tiles:
                runs[-1][1] += 1
            else:
                runs.append([other, 1])
        steps += [(block_no, start, tiles) for start, tiles in runs]
    return steps


def near_blocks(first, count, row_features, column_features, sides_t, total, kernels):
    steps = near_steps(first, count, column_features.shape[1] // block)
    own = {}

    def entries(step_no):
        block_no, start, tiles = steps[step_no]
        columns = pl.ds(start * block, tiles * block)
        rows = pl.ds(block_no * block, block)
        squared = jnp.dot(row_features[rows, :], column_features[:, columns], preferred_element_type=f32)
        squared = jnp.maximum(squared, 1e-30)
        scaled = squared * lax.rsqrt(squared)
        kernel = (1.0 + log_two * scaled) * jnp.exp2(-scaled)
        kernels[step_no % 2, :, pl.ds(0, tiles * block)] = kernel.astype(bf16)

    def products(step_no):
        block_no, start, tiles = steps[step_no]
        columns = pl.ds(start * block, tiles * block)
        rows = pl.ds(block_no * block, block)
        kernel = kernels[step_no % 2, :, pl.ds(0, tiles * block)]
        part = lax.dot_general(
            sides_t[:, columns], kernel, (((1,), (1,)), ((), ())), preferred_element_type=f32
        )
        own[block_no] = own[block_no] + part if block_no in own else part
        if start != block_no:
            total[:, columns] += jnp.dot(sides_t[:, rows], kernel, preferred_element_type=f32)
        if step_no + 1 == len(steps) or steps[step_no + 1][0] != block_no:
            total[:, rows] += own.pop(block_no)

    for step_no in range(len(steps) + 1):
        if step_no < len(steps):
            entries(step_no)
            yield
        if step_no:
            products(step_no - 1)
            yield


def near_kernel(first, count, arrivals, row_features, column_features, sides_t, matrices, *refs):
    refs = list(refs)
    before = refs.pop(0)
    mixed, total, kernels = refs[-3:]
    points = column_features.shape[1]
    position = 0
    for slot, (level_no, number) in enumerate(arrivals):
        mixed[slot] = mix(matrices, level_no, refs[position : position + number], points)
        position += number
    total[...] = before[...]
    for _ in near_blocks(first, count, row_features, column_features, sides_t, total, kernels):
        pass


def select_rows(own, couplings, matrices):
    levels, rank, _ = matrices.shape
    nodes = couplings.shape[2]
    lane = lax.broadcasted_iota(jnp.int32, (8, nodes), 1)
    level = lax.broadcasted_iota(jnp.int32, (8, nodes), 0)
    leaf = own[0]
    chosen = jnp.zeros((8, nodes), f32)
    for level_no in range(levels):
        node = (nodes + 1 >> level_no + 1) + (leaf >> level_no + 1) - 1
        chosen = jnp.where((level == level_no) & (lane == node), 1.0, chosen)
    chosen = chosen.astype(bf16)
    for row in range(rank):
        taken = sum(
            lax.dot_general(chosen, part.astype(bf16), (((1,), (1,)), ((), ())), preferred_element_type=f32)
            for part in split_three(couplings[row])
        )
        for level_no in range(levels):
            matrices[level_no, pl.ds(row, 1), :] = taken[level_no : level_no + 1, :]
        yield
    for level_no in range(levels):
        matrix = matrices[level_no]
        second = (leaf >> level_no & 1) == 1
        matrices[level_no] = jnp.where(second, matrix.T, matrix)


def first_kernel(count, own, row_features, column_features, sides_t, couplings, matrices, total, kernels):
    total[...] = jnp.zeros_like(total)
    picks = select_rows(own, couplings, matrices)
    for _ in near_blocks(0, count, row_features, column_features, sides_t, total, kernels):
        next(picks, None)
    for _ in picks:
        pass


def first_part(count, own, features, couplings, levels):
    width, points = features[2].shape
    rank = couplings.shape[0]
    entries = count * block * points // 2
    return pl.pallas_call(
        functools.partial(first_kernel, count),
        out_shape=[
            jax.ShapeDtypeStruct((levels, rank, rank), f32),
            jax.ShapeDtypeStruct((width, points), f32),
        ],
        in_specs=[smem] + [vmem] * 4,
        out_specs=[vmem, vmem],
        scratch_shapes=[pltpu.VMEM((2, block, group_tiles * block), bf16)],
        compiler_params=params(16),
        cost_estimate=pl.CostEstimate(
            flops=entries * 6 * width, bytes_accessed=6 * 10**6, transcendentals=2 * entries
        ),
        name="first_part",
    )(own, *features, couplings)


def near_part(first, count, features, matrices, before, arrivals):
    width, points = features[2].shape
    rank = matrices.shape[1]
    entries = count * block * points // 2
    arrived = [array for _, arrays in arrivals for array in arrays]
    counts = tuple((level_no, len(arrays)) for level_no, arrays in arrivals)
    return pl.pallas_call(
        functools.partial(near_kernel, first, count, counts),
        out_shape=[
            jax.ShapeDtypeStruct((len(arrivals), rank, width), bf16),
            jax.ShapeDtypeStruct((width, points), f32),
        ],
        in_specs=[vmem] * (5 + len(arrived)),
        out_specs=[vmem, vmem],
        scratch_shapes=[pltpu.VMEM((2, block, group_tiles * block), bf16)],
        input_output_aliases={4: 1},
        compiler_params=params(16),
        cost_estimate=pl.CostEstimate(
            flops=entries * 6 * width, bytes_accessed=6 * 10**6, transcendentals=2 * entries
        ),
        name="near_part",
    )(*features, matrices, before, *arrived)


def tail_kernel(arrivals, first, order_in, before, bases, matrices, row_features, column_features, sides_t, *refs):
    refs = list(refs)
    out, order, total, kernels, placed, order_sem, out_sems, *far_rows = refs[-(7 + before.shape[1] // chunk) :]
    refs = refs[: -(7 + len(far_rows))]
    points = before.shape[1]
    copy = pltpu.make_async_copy(order_in, order, order_sem)
    copy.start()
    arrived = refs[: sum(number for _, number in arrivals)]
    mixed = [earlier[slot] for earlier in refs[len(arrived) :] for slot in range(earlier.shape[0])]
    position = 0
    for level_no, number in arrivals:
        mixed.append(mix(matrices, level_no, arrived[position : position + number], points))
        position += number
    mixed_t = jnp.concatenate(mixed, axis=0).astype(f32).T.astype(bf16)
    copy.wait()

    def far(chunk_no):
        columns = pl.ds(chunk_no * chunk, chunk)
        far_rows[chunk_no][...] = jnp.dot(mixed_t, bases[:, columns], preferred_element_type=f32).T

    def scatter(first_row, last_row):
        for row in range(first_row, last_row):
            value = far_rows[row // chunk][pl.ds(row % chunk, 1), :]
            placed[pl.ds(order[0, row], 1), :] = value

    total[...] = before[...]
    blocks = points // block
    near = near_blocks(first, blocks - first, row_features, column_features, sides_t, total, kernels)
    far(0)
    share = chunk // 4
    for row in range(0, points, share):
        if row % chunk == 0 and row + chunk < points:
            far(row // chunk + 1)
        scatter(row, row + share)
        next(near, None)
    for _ in near:
        pass
    copies = []
    for part in range(out_sems.shape[0]):
        rows = pl.ds(part * chunk, chunk)
        placed[rows, :] += kernel_amplitude * total[:, rows].T
        copies.append(pltpu.make_async_copy(placed.at[rows, :], out.at[rows, :], out_sems.at[part]))
        copies[-1].start()
    for copy in copies:
        copy.wait()


def tail(order, near_t, flat_bases, matrices, features, first, mixed, arrivals):
    width, points = near_t.shape
    arrived = [array for _, arrays in arrivals for array in arrays]
    counts = tuple((level_no, len(arrays)) for level_no, arrays in arrivals)
    dma = pltpu.SemaphoreType.DMA
    return pl.pallas_call(
        functools.partial(tail_kernel, counts, first),
        out_shape=jax.ShapeDtypeStruct((points, width), f32),
        in_specs=[hbm] + [vmem] * (6 + len(arrived) + len(mixed)),
        out_specs=hbm,
        scratch_shapes=[
            pltpu.SMEM(order.shape, jnp.int32),
            pltpu.VMEM((width, points), f32),
            pltpu.VMEM((2, block, group_tiles * block), bf16),
            pltpu.VMEM((points, width), f32),
            dma,
            dma((points // chunk,)),
        ]
        + [pltpu.VMEM((chunk, width), f32)] * (points // chunk),
        compiler_params=params(20),
        cost_estimate=pl.CostEstimate(flops=9 * 10**9, bytes_accessed=5 * 10**6, transcendentals=0),
        name="tail",
    )(order, near_t, flat_bases, matrices, *features, *arrived, *mixed)


def local(right_sides, coords, cluster_order, bases, coupling):
    levels, rank, points = bases.shape
    leaves = lax.axis_size("leaf")
    own = lax.axis_index("leaf").astype(jnp.int32).reshape(1)
    flat_bases = bases.reshape(levels * rank, points)

    def exchange(sent, mask):
        return lax.ppermute(sent, "leaf", [(leaf, leaf ^ mask) for leaf in range(leaves)])

    couplings = jnp.transpose(coupling, (1, 2, 0))
    held, sides, points_held, couplings = gather_project(
        cluster_order, right_sides, flat_bases, coords, couplings, levels
    )
    got = exchange(held, 1)
    features = prepare(points_held, sides)
    got, *features = lax.optimization_barrier((got, *features))
    arrivals = [(0, [got])]
    held = held[1:] + got[1:]
    first, mixed = 0, []
    for axis_no, (step, count) in enumerate(zip(axis_steps, near_shares)):
        last = axis_no == len(axis_steps) - 1
        near_side = exchange(held[:1] if last else held, step)
        across = exchange(held[1:], 2 * step)
        corner = exchange(held[1:], 3 * step)
        features[1], held = lax.optimization_barrier((features[1], held))
        if axis_no == 0:
            matrices, near_t = first_part(count, own, features, couplings, levels)
        else:
            mixed_part, near_t = near_part(first, count, features, matrices, near_t, arrivals)
            mixed.append(mixed_part)
            arrivals = []
        first += count
        near_side, across, corner, near_t = lax.optimization_barrier((near_side, across, corner, near_t))
        arrivals = arrivals + [(2 * axis_no + 1, [near_side]), (2 * axis_no + 2, [across, corner])]
        if not last:
            held = (held[2:] + near_side[2:]) + (across[1:] + corner[1:])
    return tail(cluster_order, near_t, flat_bases, matrices, features, first, mixed, arrivals)


def solution(mesh):
    in_specs = (P("leaf", None), P(None, "leaf"), P("leaf", None), P(None, None, "leaf"), P())
    out_specs = P("leaf", None)
    return jax.shard_map(local, mesh=mesh, in_specs=in_specs, out_specs=out_specs, check_vma=False)
```

```python
import functools
import math

import jax
import jax.numpy as jnp
from jax import lax
from jax.experimental import pallas as pl
from jax.experimental.pallas import tpu as pltpu
from jax.sharding import PartitionSpec as P

length_scale = 0.25
kernel_amplitude = 0.25
root_three = math.sqrt(3.0)
log_two = math.log(2.0)
point_scale = root_three / length_scale / log_two
block = 256
group_tiles = 2
feature_rows = 32
chunk = 512
near_shares = (6, 5, 3)
axis_steps = (2, 8, 32)

vmem = pl.BlockSpec(memory_space=pltpu.VMEM)
smem = pl.BlockSpec(memory_space=pltpu.SMEM)
hbm = pl.BlockSpec(memory_space=pltpu.HBM)
f32, bf16 = jnp.float32, jnp.bfloat16


def params(mib):
    return pltpu.CompilerParams(vmem_limit_bytes=mib * 2**20)


def split_three(wide):
    high = wide.astype(bf16).astype(f32)
    middle = (wide - high).astype(bf16).astype(f32)
    return high, middle, wide - high - middle


def gather_kernel(order_in, sides_in, bases_in, coords_in, couplings_in, *refs):
    projected, sides, coords, couplings, order, bases, wide, first_sems, base_sems, other_sems, *values = refs
    points = sides.shape[0]
    levels = projected.shape[0]
    chunks = len(values)
    quarter = points // 4
    first_copies = [pltpu.make_async_copy(order_in, order, first_sems.at[0])]
    for part in range(4):
        rows = pl.ds(part * quarter, quarter)
        first_copies.append(pltpu.make_async_copy(sides_in.at[rows, :], sides.at[rows, :], first_sems.at[part + 1]))
    rank = bases.shape[0] // levels
    base_copies = []
    for part in range(levels):
        rows = pl.ds(part * rank, rank)
        base_copies.append(pltpu.make_async_copy(bases_in.at[rows, :], bases.at[rows, :], base_sems.at[part]))
    other_copies = [
        pltpu.make_async_copy(coords_in, coords, other_sems.at[0]),
        pltpu.make_async_copy(couplings_in, couplings, other_sems.at[1]),
    ]
    for copy in first_copies:
        copy.start()
    for part, copy in enumerate(first_copies):
        copy.wait()
        if part:
            rows = pl.ds((part - 1) * quarter, quarter)
            wide[rows, :] = sides[rows, :].astype(f32)
    for copy in base_copies + other_copies:
        copy.start()

    def take(chunk_no):
        for row in range(chunk):
            place = order[0, chunk_no * chunk + row]
            values[chunk_no][pl.ds(row, 1), :] = wide[pl.ds(place, 1), :]

    def project(first, last):
        taken = jnp.concatenate([values[chunk_no][...].astype(bf16) for chunk_no in range(first, last)], axis=0)
        columns = pl.ds(first * chunk, (last - first) * chunk)
        part = jnp.dot(bases[:, columns], taken, preferred_element_type=f32).reshape(projected.shape)
        if first:
            projected[...] += part
        else:
            projected[...] = part

    for chunk_no in range(chunks):
        if chunk_no == chunks - 3:
            for copy in base_copies:
                copy.wait()
            project(0, chunks - 4)
        if chunk_no == chunks - 1:
            project(chunks - 4, chunks - 2)
        take(chunk_no)
    project(chunks - 2, chunks)
    for copy in other_copies:
        copy.wait()


def gather_project(order, sides, flat_bases, coords, couplings, levels):
    points, width = sides.shape
    dma = pltpu.SemaphoreType.DMA
    inputs = (order, sides, flat_bases, coords, couplings)
    return pl.pallas_call(
        gather_kernel,
        out_shape=[
            pltpu.VMEM((levels, flat_bases.shape[0] // levels, width), f32),
            pltpu.VMEM(sides.shape, bf16),
            pltpu.VMEM(coords.shape, f32),
            pltpu.VMEM(couplings.shape, f32),
        ],
        in_specs=[hbm] * 5,
        out_specs=[vmem] * 4,
        scratch_shapes=[
            pltpu.SMEM(order.shape, jnp.int32),
            pltpu.VMEM(flat_bases.shape, bf16),
            pltpu.VMEM((points, width), f32),
            dma((5,)),
            dma((levels,)),
            dma((2,)),
        ]
        + [pltpu.VMEM((chunk, width), f32)] * (points // chunk),
        compiler_params=params(32),
        cost_estimate=pl.CostEstimate(flops=7 * 10**9, bytes_accessed=5 * 10**6, transcendentals=0),
        name="gather_project",
    )(*(pltpu.with_memory_space_constraint(array, pltpu.HBM) for array in inputs))


def prepare_kernel(coords, sides, row_features, column_features, sides_t):
    points = coords.shape[1]
    placed = (coords[...] - 0.5) * point_scale
    high, middle, low = split_three(placed)
    norm_parts = split_three(jnp.sum(placed * placed, axis=0, keepdims=True))
    ones = [jnp.ones((1, points), f32)] * 3
    filler = jnp.zeros((feature_rows - 24, points), f32)
    row_side = [-2 * high, -2 * high, -2 * middle, -2 * middle, -2 * high, -2 * low, *norm_parts, *ones, filler]
    column_side = [high, middle, high, middle, low, high, *ones, *norm_parts, filler]
    row_features[...] = jnp.concatenate(row_side, axis=0).T.astype(bf16)
    column_features[...] = jnp.concatenate(column_side, axis=0).astype(bf16)
    sides_t[...] = sides[...].astype(f32).T.astype(bf16)


def prepare(coords, sides):
    points, width = sides.shape
    return pl.pallas_call(
        prepare_kernel,
        out_shape=[
            pltpu.VMEM((points, feature_rows), bf16),
            pltpu.VMEM((feature_rows, points), bf16),
            pltpu.VMEM((width, points), bf16),
        ],
        in_specs=[vmem] * 2,
        out_specs=[vmem] * 3,
        compiler_params=params(16),
        cost_estimate=pl.CostEstimate(flops=3 * 10**9, bytes_accessed=3 * 10**6, transcendentals=0),
        name="prepare",
    )(*(pltpu.with_memory_space_constraint(array, pltpu.VMEM) for array in (coords, sides)))


def mix(matrices, level_no, arrived, points):
    sibling = arrived[0][0]
    for other in arrived[1:]:
        sibling = sibling + other[0]
    factor_scale = 1.0 / math.sqrt(2**level_no * points)
    return jnp.dot(
        matrices[level_no], sibling * factor_scale, precision=lax.Precision.HIGHEST, preferred_element_type=f32
    ).astype(bf16)


def near_steps(first, count, blocks):
    half = blocks // 2
    steps = []
    for block_no in range(first, first + count):
        runs = [[block_no, 1]]
        for step in range(1, half + 1 if block_no < half else half):
            other = (block_no + step) % blocks
            if len(runs) > 1 and sum(runs[-1]) == other and runs[-1][1] < group_tiles:
                runs[-1][1] += 1
            else:
                runs.append([other, 1])
        steps += [(block_no, start, tiles) for start, tiles in runs]
    return steps


def near_blocks(first, count, row_features, column_features, sides_t, total, kernels):
    steps = near_steps(first, count, column_features.shape[1] // block)
    own = {}

    def entries(step_no):
        block_no, start, tiles = steps[step_no]
        columns = pl.ds(start * block, tiles * block)
        rows = pl.ds(block_no * block, block)
        squared = jnp.dot(row_features[rows, :], column_features[:, columns], preferred_element_type=f32)
        squared = jnp.maximum(squared, 1e-30)
        scaled = squared * lax.rsqrt(squared)
        kernel = (1.0 + log_two * scaled) * jnp.exp2(-scaled)
        kernels[step_no % 2, :, pl.ds(0, tiles * block)] = kernel.astype(bf16)

    def products(step_no):
        block_no, start, tiles = steps[step_no]
        columns = pl.ds(start * block, tiles * block)
        rows = pl.ds(block_no * block, block)
        kernel = kernels[step_no % 2, :, pl.ds(0, tiles * block)]
        part = lax.dot_general(
            sides_t[:, columns], kernel, (((1,), (1,)), ((), ())), preferred_element_type=f32
        )
        own[block_no] = own[block_no] + part if block_no in own else part
        if start != block_no:
            total[:, columns] += jnp.dot(sides_t[:, rows], kernel, preferred_element_type=f32)
        if step_no + 1 == len(steps) or steps[step_no + 1][0] != block_no:
            total[:, rows] += own.pop(block_no)

    for step_no in range(len(steps) + 1):
        if step_no < len(steps):
            entries(step_no)
            yield
        if step_no:
            products(step_no - 1)
            yield


def near_kernel(first, count, arrivals, row_features, column_features, sides_t, matrices, *refs):
    refs = list(refs)
    before = refs.pop(0)
    mixed, total, kernels = refs[-3:]
    points = column_features.shape[1]
    position = 0
    for slot, (level_no, number) in enumerate(arrivals):
        mixed[slot] = mix(matrices, level_no, refs[position : position + number], points)
        position += number
    total[...] = before[...]
    for _ in near_blocks(first, count, row_features, column_features, sides_t, total, kernels):
        pass


def select_rows(own, couplings, matrices):
    levels, rank, _ = matrices.shape
    nodes = couplings.shape[2]
    lane = lax.broadcasted_iota(jnp.int32, (8, nodes), 1)
    level = lax.broadcasted_iota(jnp.int32, (8, nodes), 0)
    leaf = own[0]
    chosen = jnp.zeros((8, nodes), f32)
    for level_no in range(levels):
        node = (nodes + 1 >> level_no + 1) + (leaf >> level_no + 1) - 1
        chosen = jnp.where((level == level_no) & (lane == node), 1.0, chosen)
    chosen = chosen.astype(bf16)
    for row in range(rank):
        taken = sum(
            lax.dot_general(chosen, part.astype(bf16), (((1,), (1,)), ((), ())), preferred_element_type=f32)
            for part in split_three(couplings[row])
        )
        for level_no in range(levels):
            matrices[level_no, pl.ds(row, 1), :] = taken[level_no : level_no + 1, :]
        yield
    for level_no in range(levels):
        matrix = matrices[level_no]
        second = (leaf >> level_no & 1) == 1
        matrices[level_no] = jnp.where(second, matrix.T, matrix)


def first_kernel(count, own, row_features, column_features, sides_t, couplings, matrices, total, kernels):
    total[...] = jnp.zeros_like(total)
    picks = select_rows(own, couplings, matrices)
    for _ in near_blocks(0, count, row_features, column_features, sides_t, total, kernels):
        next(picks, None)
    for _ in picks:
        pass


def first_part(count, own, features, couplings, levels):
    width, points = features[2].shape
    rank = couplings.shape[0]
    entries = count * block * points // 2
    return pl.pallas_call(
        functools.partial(first_kernel, count),
        out_shape=[
            jax.ShapeDtypeStruct((levels, rank, rank), f32),
            jax.ShapeDtypeStruct((width, points), f32),
        ],
        in_specs=[smem] + [vmem] * 4,
        out_specs=[vmem, vmem],
        scratch_shapes=[pltpu.VMEM((2, block, group_tiles * block), bf16)],
        compiler_params=params(16),
        cost_estimate=pl.CostEstimate(
            flops=entries * 6 * width, bytes_accessed=6 * 10**6, transcendentals=2 * entries
        ),
        name="first_part",
    )(own, *features, pltpu.with_memory_space_constraint(couplings, pltpu.VMEM))


def near_part(first, count, features, matrices, before, arrivals):
    width, points = features[2].shape
    rank = matrices.shape[1]
    entries = count * block * points // 2
    arrived = [array for _, arrays in arrivals for array in arrays]
    counts = tuple((level_no, len(arrays)) for level_no, arrays in arrivals)
    return pl.pallas_call(
        functools.partial(near_kernel, first, count, counts),
        out_shape=[
            jax.ShapeDtypeStruct((len(arrivals), rank, width), bf16),
            jax.ShapeDtypeStruct((width, points), f32),
        ],
        in_specs=[vmem] * (5 + len(arrived)),
        out_specs=[vmem, vmem],
        scratch_shapes=[pltpu.VMEM((2, block, group_tiles * block), bf16)],
        input_output_aliases={4: 1},
        compiler_params=params(16),
        cost_estimate=pl.CostEstimate(
            flops=entries * 6 * width, bytes_accessed=6 * 10**6, transcendentals=2 * entries
        ),
        name="near_part",
    )(*features, matrices, before, *arrived)


def tail_kernel(arrivals, first, order_in, before, bases, matrices, row_features, column_features, sides_t, *refs):
    refs = list(refs)
    out, order, total, kernels, placed, order_sem, out_sems, *far_rows = refs[-(7 + before.shape[1] // chunk) :]
    refs = refs[: -(7 + len(far_rows))]
    points = before.shape[1]
    copy = pltpu.make_async_copy(order_in, order, order_sem)
    copy.start()
    arrived = refs[: sum(number for _, number in arrivals)]
    mixed = [earlier[slot] for earlier in refs[len(arrived) :] for slot in range(earlier.shape[0])]
    position = 0
    for level_no, number in arrivals:
        mixed.append(mix(matrices, level_no, arrived[position : position + number], points))
        position += number
    mixed_t = jnp.concatenate(mixed, axis=0).astype(f32).T.astype(bf16)
    copy.wait()

    def far(chunk_no):
        columns = pl.ds(chunk_no * chunk, chunk)
        far_rows[chunk_no][...] = jnp.dot(mixed_t, bases[:, columns], preferred_element_type=f32).T

    def scatter(first_row, last_row):
        for row in range(first_row, last_row):
            value = far_rows[row // chunk][pl.ds(row % chunk, 1), :]
            placed[pl.ds(order[0, row], 1), :] = value

    total[...] = before[...]
    blocks = points // block
    near = near_blocks(first, blocks - first, row_features, column_features, sides_t, total, kernels)
    far(0)
    share = chunk // 4
    for row in range(0, points, share):
        if row % chunk == 0 and row + chunk < points:
            far(row // chunk + 1)
        scatter(row, row + share)
        next(near, None)
    for _ in near:
        pass
    copies = []
    for part in range(out_sems.shape[0]):
        rows = pl.ds(part * chunk, chunk)
        placed[rows, :] += kernel_amplitude * total[:, rows].T
        copies.append(pltpu.make_async_copy(placed.at[rows, :], out.at[rows, :], out_sems.at[part]))
        copies[-1].start()
    for copy in copies:
        copy.wait()


def tail(order, near_t, flat_bases, matrices, features, first, mixed, arrivals):
    width, points = near_t.shape
    arrived = [array for _, arrays in arrivals for array in arrays]
    counts = tuple((level_no, len(arrays)) for level_no, arrays in arrivals)
    dma = pltpu.SemaphoreType.DMA
    return pl.pallas_call(
        functools.partial(tail_kernel, counts, first),
        out_shape=jax.ShapeDtypeStruct((points, width), f32),
        in_specs=[hbm] + [vmem] * (6 + len(arrived) + len(mixed)),
        out_specs=hbm,
        scratch_shapes=[
            pltpu.SMEM(order.shape, jnp.int32),
            pltpu.VMEM((width, points), f32),
            pltpu.VMEM((2, block, group_tiles * block), bf16),
            pltpu.VMEM((points, width), f32),
            dma,
            dma((points // chunk,)),
        ]
        + [pltpu.VMEM((chunk, width), f32)] * (points // chunk),
        compiler_params=params(20),
        cost_estimate=pl.CostEstimate(flops=9 * 10**9, bytes_accessed=5 * 10**6, transcendentals=0),
        name="tail",
    )(order, near_t, flat_bases, matrices, *features, *arrived, *mixed)


def local(right_sides, coords, cluster_order, bases, coupling):
    levels, rank, points = bases.shape
    leaves = lax.axis_size("leaf")
    own = lax.axis_index("leaf").astype(jnp.int32).reshape(1)
    flat_bases = bases.reshape(levels * rank, points)

    def exchange(sent, mask):
        return lax.ppermute(sent, "leaf", [(leaf, leaf ^ mask) for leaf in range(leaves)])

    couplings = jnp.transpose(coupling, (1, 2, 0))
    held, sides, points_held, couplings = gather_project(
        cluster_order, right_sides, flat_bases, coords, couplings, levels
    )
    got = exchange(held, 1)
    features = prepare(points_held, sides)
    got, *features = lax.optimization_barrier((got, *features))
    arrivals = [(0, [got])]
    held = held[1:] + got[1:]
    first, mixed = 0, []
    for axis_no, (step, count) in enumerate(zip(axis_steps, near_shares)):
        last = axis_no == len(axis_steps) - 1
        near_side = exchange(held[:1] if last else held, step)
        across = exchange(held[1:], 2 * step)
        corner = exchange(held[1:], 3 * step)
        features[1], held = lax.optimization_barrier((features[1], held))
        if axis_no == 0:
            matrices, near_t = first_part(count, own, features, couplings, levels)
        else:
            mixed_part, near_t = near_part(first, count, features, matrices, near_t, arrivals)
            mixed.append(mixed_part)
            arrivals = []
        first += count
        near_side, across, corner, near_t = lax.optimization_barrier((near_side, across, corner, near_t))
        arrivals = arrivals + [(2 * axis_no + 1, [near_side]), (2 * axis_no + 2, [across, corner])]
        if not last:
            held = (held[2:] + near_side[2:]) + (across[1:] + corner[1:])
    return tail(cluster_order, near_t, flat_bases, matrices, features, first, mixed, arrivals)


def solution(mesh):
    in_specs = (P("leaf", None), P(None, "leaf"), P("leaf", None), P(None, None, "leaf"), P())
    out_specs = P("leaf", None)
    return jax.shard_map(local, mesh=mesh, in_specs=in_specs, out_specs=out_specs, check_vma=False)
```

```python
import functools
import math

import jax
import jax.numpy as jnp
from jax import lax
from jax.experimental import pallas as pl
from jax.experimental.pallas import tpu as pltpu
from jax.sharding import PartitionSpec as P

length_scale = 0.25
kernel_amplitude = 0.25
root_three = math.sqrt(3.0)
log_two = math.log(2.0)
point_scale = root_three / length_scale / log_two
block = 256
group_tiles = 2
feature_rows = 32
chunk = 512
near_shares = (6, 5, 3)
axis_steps = (2, 8, 32)

vmem = pl.BlockSpec(memory_space=pltpu.VMEM)
smem = pl.BlockSpec(memory_space=pltpu.SMEM)
hbm = pl.BlockSpec(memory_space=pltpu.HBM)
f32, bf16 = jnp.float32, jnp.bfloat16


def params(mib):
    return pltpu.CompilerParams(vmem_limit_bytes=mib * 2**20)


def split_three(wide):
    high = wide.astype(bf16).astype(f32)
    middle = (wide - high).astype(bf16).astype(f32)
    return high, middle, wide - high - middle


def gather_kernel(order_in, sides_in, bases_in, coords_in, couplings_in, *refs):
    projected, coords, couplings, order, sides, bases, wide, first_sems, base_sems, other_sems, *values = refs
    points = sides.shape[0]
    levels = projected.shape[0]
    chunks = len(values)
    quarter = points // 4
    first_copies = [pltpu.make_async_copy(order_in, order, first_sems.at[0])]
    for part in range(4):
        rows = pl.ds(part * quarter, quarter)
        first_copies.append(pltpu.make_async_copy(sides_in.at[rows, :], sides.at[rows, :], first_sems.at[part + 1]))
    rank = bases.shape[0] // levels
    base_copies = []
    for part in range(levels):
        rows = pl.ds(part * rank, rank)
        base_copies.append(pltpu.make_async_copy(bases_in.at[rows, :], bases.at[rows, :], base_sems.at[part]))
    other_copies = [
        pltpu.make_async_copy(coords_in, coords, other_sems.at[0]),
        pltpu.make_async_copy(couplings_in, couplings, other_sems.at[1]),
    ]
    for copy in first_copies:
        copy.start()
    for part, copy in enumerate(first_copies):
        copy.wait()
        if part:
            rows = pl.ds((part - 1) * quarter, quarter)
            wide[rows, :] = sides[rows, :].astype(f32)
    for copy in base_copies + other_copies:
        copy.start()

    def take(chunk_no):
        for row in range(chunk):
            place = order[0, chunk_no * chunk + row]
            values[chunk_no][pl.ds(row, 1), :] = wide[pl.ds(place, 1), :]

    def project(first, last):
        taken = jnp.concatenate([values[chunk_no][...].astype(bf16) for chunk_no in range(first, last)], axis=0)
        columns = pl.ds(first * chunk, (last - first) * chunk)
        part = jnp.dot(bases[:, columns], taken, preferred_element_type=f32).reshape(projected.shape)
        if first:
            projected[...] += part
        else:
            projected[...] = part

    for chunk_no in range(chunks):
        if chunk_no == chunks - 3:
            for copy in base_copies:
                copy.wait()
            project(0, chunks - 4)
        if chunk_no == chunks - 1:
            project(chunks - 4, chunks - 2)
        take(chunk_no)
    project(chunks - 2, chunks)
    for copy in other_copies:
        copy.wait()


def gather_project(order, sides, flat_bases, coords, couplings, levels):
    points, width = sides.shape
    dma = pltpu.SemaphoreType.DMA
    inputs = (order, sides, flat_bases, coords, couplings)
    return pl.pallas_call(
        gather_kernel,
        out_shape=[
            pltpu.VMEM((levels, flat_bases.shape[0] // levels, width), f32),
            pltpu.VMEM(coords.shape, f32),
            pltpu.VMEM(couplings.shape, f32),
        ],
        in_specs=[hbm] * 5,
        out_specs=[vmem] * 3,
        scratch_shapes=[
            pltpu.SMEM(order.shape, jnp.int32),
            pltpu.VMEM(sides.shape, bf16),
            pltpu.VMEM(flat_bases.shape, bf16),
            pltpu.VMEM((points, width), f32),
            dma((5,)),
            dma((levels,)),
            dma((2,)),
        ]
        + [pltpu.VMEM((chunk, width), f32)] * (points // chunk),
        compiler_params=params(32),
        cost_estimate=pl.CostEstimate(flops=7 * 10**9, bytes_accessed=5 * 10**6, transcendentals=0),
        name="gather_project",
    )(*(pltpu.with_memory_space_constraint(array, pltpu.HBM) for array in inputs))


def prepare_kernel(coords, sides_in, row_features, column_features, sides_t, sides, side_sem):
    copy = pltpu.make_async_copy(sides_in, sides, side_sem)
    copy.start()
    points = coords.shape[1]
    placed = (coords[...] - 0.5) * point_scale
    high, middle, low = split_three(placed)
    norm_parts = split_three(jnp.sum(placed * placed, axis=0, keepdims=True))
    ones = [jnp.ones((1, points), f32)] * 3
    filler = jnp.zeros((feature_rows - 24, points), f32)
    row_side = [-2 * high, -2 * high, -2 * middle, -2 * middle, -2 * high, -2 * low, *norm_parts, *ones, filler]
    column_side = [high, middle, high, middle, low, high, *ones, *norm_parts, filler]
    row_features[...] = jnp.concatenate(row_side, axis=0).T.astype(bf16)
    column_features[...] = jnp.concatenate(column_side, axis=0).astype(bf16)
    copy.wait()
    sides_t[...] = sides[...].astype(f32).T.astype(bf16)


def prepare(coords, sides):
    points, width = sides.shape
    return pl.pallas_call(
        prepare_kernel,
        out_shape=[
            pltpu.VMEM((points, feature_rows), bf16),
            pltpu.VMEM((feature_rows, points), bf16),
            pltpu.VMEM((width, points), bf16),
        ],
        in_specs=[vmem, hbm],
        out_specs=[vmem] * 3,
        scratch_shapes=[pltpu.VMEM(sides.shape, bf16), pltpu.SemaphoreType.DMA],
        compiler_params=params(16),
        cost_estimate=pl.CostEstimate(flops=3 * 10**9, bytes_accessed=3 * 10**6, transcendentals=0),
        name="prepare",
    )(coords, pltpu.with_memory_space_constraint(sides, pltpu.HBM))


def mix(matrices, level_no, arrived, points):
    sibling = arrived[0][0]
    for other in arrived[1:]:
        sibling = sibling + other[0]
    factor_scale = 1.0 / math.sqrt(2**level_no * points)
    return jnp.dot(
        matrices[level_no], sibling * factor_scale, precision=lax.Precision.HIGHEST, preferred_element_type=f32
    ).astype(bf16)


def near_steps(first, count, blocks):
    half = blocks // 2
    steps = []
    for block_no in range(first, first + count):
        runs = [[block_no, 1]]
        for step in range(1, half + 1 if block_no < half else half):
            other = (block_no + step) % blocks
            if len(runs) > 1 and sum(runs[-1]) == other and runs[-1][1] < group_tiles:
                runs[-1][1] += 1
            else:
                runs.append([other, 1])
        steps += [(block_no, start, tiles) for start, tiles in runs]
    return steps


def near_blocks(first, count, row_features, column_features, sides_t, total, kernels):
    steps = near_steps(first, count, column_features.shape[1] // block)
    own = {}

    def entries(step_no):
        block_no, start, tiles = steps[step_no]
        columns = pl.ds(start * block, tiles * block)
        rows = pl.ds(block_no * block, block)
        squared = jnp.dot(row_features[rows, :], column_features[:, columns], preferred_element_type=f32)
        squared = jnp.maximum(squared, 1e-30)
        scaled = squared * lax.rsqrt(squared)
        kernel = (1.0 + log_two * scaled) * jnp.exp2(-scaled)
        kernels[step_no % 2, :, pl.ds(0, tiles * block)] = kernel.astype(bf16)

    def products(step_no):
        block_no, start, tiles = steps[step_no]
        columns = pl.ds(start * block, tiles * block)
        rows = pl.ds(block_no * block, block)
        kernel = kernels[step_no % 2, :, pl.ds(0, tiles * block)]
        part = lax.dot_general(
            sides_t[:, columns], kernel, (((1,), (1,)), ((), ())), preferred_element_type=f32
        )
        own[block_no] = own[block_no] + part if block_no in own else part
        if start != block_no:
            total[:, columns] += jnp.dot(sides_t[:, rows], kernel, preferred_element_type=f32)
        if step_no + 1 == len(steps) or steps[step_no + 1][0] != block_no:
            total[:, rows] += own.pop(block_no)

    for step_no in range(len(steps) + 1):
        if step_no < len(steps):
            entries(step_no)
            yield
        if step_no:
            products(step_no - 1)
            yield


def near_kernel(first, count, arrivals, row_features, column_features, sides_t, matrices, *refs):
    refs = list(refs)
    before = refs.pop(0)
    mixed, total, kernels = refs[-3:]
    points = column_features.shape[1]
    position = 0
    for slot, (level_no, number) in enumerate(arrivals):
        mixed[slot] = mix(matrices, level_no, refs[position : position + number], points)
        position += number
    total[...] = before[...]
    for _ in near_blocks(first, count, row_features, column_features, sides_t, total, kernels):
        pass


def select_rows(own, couplings, matrices):
    levels, rank, _ = matrices.shape
    nodes = couplings.shape[2]
    lane = lax.broadcasted_iota(jnp.int32, (8, nodes), 1)
    level = lax.broadcasted_iota(jnp.int32, (8, nodes), 0)
    leaf = own[0]
    chosen = jnp.zeros((8, nodes), f32)
    for level_no in range(levels):
        node = (nodes + 1 >> level_no + 1) + (leaf >> level_no + 1) - 1
        chosen = jnp.where((level == level_no) & (lane == node), 1.0, chosen)
    chosen = chosen.astype(bf16)
    for row in range(rank):
        taken = sum(
            lax.dot_general(chosen, part.astype(bf16), (((1,), (1,)), ((), ())), preferred_element_type=f32)
            for part in split_three(couplings[row])
        )
        for level_no in range(levels):
            matrices[level_no, pl.ds(row, 1), :] = taken[level_no : level_no + 1, :]
        yield
    for level_no in range(levels):
        matrix = matrices[level_no]
        second = (leaf >> level_no & 1) == 1
        matrices[level_no] = jnp.where(second, matrix.T, matrix)


def first_kernel(count, own, row_features, column_features, sides_t, couplings, matrices, total, kernels):
    total[...] = jnp.zeros_like(total)
    picks = select_rows(own, couplings, matrices)
    for _ in near_blocks(0, count, row_features, column_features, sides_t, total, kernels):
        next(picks, None)
    for _ in picks:
        pass


def first_part(count, own, features, couplings, levels):
    width, points = features[2].shape
    rank = couplings.shape[0]
    entries = count * block * points // 2
    return pl.pallas_call(
        functools.partial(first_kernel, count),
        out_shape=[
            jax.ShapeDtypeStruct((levels, rank, rank), f32),
            jax.ShapeDtypeStruct((width, points), f32),
        ],
        in_specs=[smem] + [vmem] * 4,
        out_specs=[vmem, vmem],
        scratch_shapes=[pltpu.VMEM((2, block, group_tiles * block), bf16)],
        compiler_params=params(16),
        cost_estimate=pl.CostEstimate(
            flops=entries * 6 * width, bytes_accessed=6 * 10**6, transcendentals=2 * entries
        ),
        name="first_part",
    )(own, *features, pltpu.with_memory_space_constraint(couplings, pltpu.VMEM))


def near_part(first, count, features, matrices, before, arrivals):
    width, points = features[2].shape
    rank = matrices.shape[1]
    entries = count * block * points // 2
    arrived = [array for _, arrays in arrivals for array in arrays]
    counts = tuple((level_no, len(arrays)) for level_no, arrays in arrivals)
    return pl.pallas_call(
        functools.partial(near_kernel, first, count, counts),
        out_shape=[
            jax.ShapeDtypeStruct((len(arrivals), rank, width), bf16),
            jax.ShapeDtypeStruct((width, points), f32),
        ],
        in_specs=[vmem] * (5 + len(arrived)),
        out_specs=[vmem, vmem],
        scratch_shapes=[pltpu.VMEM((2, block, group_tiles * block), bf16)],
        input_output_aliases={4: 1},
        compiler_params=params(16),
        cost_estimate=pl.CostEstimate(
            flops=entries * 6 * width, bytes_accessed=6 * 10**6, transcendentals=2 * entries
        ),
        name="near_part",
    )(*features, matrices, before, *arrived)


def tail_kernel(arrivals, first, order_in, before, bases, matrices, row_features, column_features, sides_t, *refs):
    refs = list(refs)
    out, order, total, kernels, placed, order_sem, out_sems, *far_rows = refs[-(7 + before.shape[1] // chunk) :]
    refs = refs[: -(7 + len(far_rows))]
    points = before.shape[1]
    copy = pltpu.make_async_copy(order_in, order, order_sem)
    copy.start()
    arrived = refs[: sum(number for _, number in arrivals)]
    mixed = [earlier[slot] for earlier in refs[len(arrived) :] for slot in range(earlier.shape[0])]
    position = 0
    for level_no, number in arrivals:
        mixed.append(mix(matrices, level_no, arrived[position : position + number], points))
        position += number
    mixed_t = jnp.concatenate(mixed, axis=0).astype(f32).T.astype(bf16)
    copy.wait()

    def far(chunk_no):
        columns = pl.ds(chunk_no * chunk, chunk)
        far_rows[chunk_no][...] = jnp.dot(mixed_t, bases[:, columns], preferred_element_type=f32).T

    def scatter(first_row, last_row):
        for row in range(first_row, last_row):
            value = far_rows[row // chunk][pl.ds(row % chunk, 1), :]
            placed[pl.ds(order[0, row], 1), :] = value

    total[...] = before[...]
    blocks = points // block
    near = near_blocks(first, blocks - first, row_features, column_features, sides_t, total, kernels)
    far(0)
    share = chunk // 4
    for row in range(0, points, share):
        if row % chunk == 0 and row + chunk < points:
            far(row // chunk + 1)
        scatter(row, row + share)
        next(near, None)
    for _ in near:
        pass
    copies = []
    for part in range(out_sems.shape[0]):
        rows = pl.ds(part * chunk, chunk)
        placed[rows, :] += kernel_amplitude * total[:, rows].T
        copies.append(pltpu.make_async_copy(placed.at[rows, :], out.at[rows, :], out_sems.at[part]))
        copies[-1].start()
    for copy in copies:
        copy.wait()


def tail(order, near_t, flat_bases, matrices, features, first, mixed, arrivals):
    width, points = near_t.shape
    arrived = [array for _, arrays in arrivals for array in arrays]
    counts = tuple((level_no, len(arrays)) for level_no, arrays in arrivals)
    dma = pltpu.SemaphoreType.DMA
    return pl.pallas_call(
        functools.partial(tail_kernel, counts, first),
        out_shape=jax.ShapeDtypeStruct((points, width), f32),
        in_specs=[hbm] + [vmem] * (6 + len(arrived) + len(mixed)),
        out_specs=hbm,
        scratch_shapes=[
            pltpu.SMEM(order.shape, jnp.int32),
            pltpu.VMEM((width, points), f32),
            pltpu.VMEM((2, block, group_tiles * block), bf16),
            pltpu.VMEM((points, width), f32),
            dma,
            dma((points // chunk,)),
        ]
        + [pltpu.VMEM((chunk, width), f32)] * (points // chunk),
        compiler_params=params(20),
        cost_estimate=pl.CostEstimate(flops=9 * 10**9, bytes_accessed=5 * 10**6, transcendentals=0),
        name="tail",
    )(order, near_t, flat_bases, matrices, *features, *arrived, *mixed)


def local(right_sides, coords, cluster_order, bases, coupling):
    levels, rank, points = bases.shape
    leaves = lax.axis_size("leaf")
    own = lax.axis_index("leaf").astype(jnp.int32).reshape(1)
    flat_bases = bases.reshape(levels * rank, points)

    def exchange(sent, mask):
        return lax.ppermute(sent, "leaf", [(leaf, leaf ^ mask) for leaf in range(leaves)])

    couplings = jnp.transpose(coupling, (1, 2, 0))
    held, placed_coords, couplings = gather_project(
        cluster_order, right_sides, flat_bases, coords, couplings, levels
    )
    got = exchange(held, 1)
    placed_coords, right_sides = lax.optimization_barrier((placed_coords, right_sides))
    features = prepare(placed_coords, right_sides)
    got, *features = lax.optimization_barrier((got, *features))
    arrivals = [(0, [got])]
    held = held[1:] + got[1:]
    first, mixed = 0, []
    for axis_no, (step, count) in enumerate(zip(axis_steps, near_shares)):
        last = axis_no == len(axis_steps) - 1
        near_side = exchange(held[:1] if last else held, step)
        across = exchange(held[1:], 2 * step)
        corner = exchange(held[1:], 3 * step)
        features[1], held = lax.optimization_barrier((features[1], held))
        if axis_no == 0:
            matrices, near_t = first_part(count, own, features, couplings, levels)
        else:
            mixed_part, near_t = near_part(first, count, features, matrices, near_t, arrivals)
            mixed.append(mixed_part)
            arrivals = []
        first += count
        near_side, across, corner, near_t = lax.optimization_barrier((near_side, across, corner, near_t))
        arrivals = arrivals + [(2 * axis_no + 1, [near_side]), (2 * axis_no + 2, [across, corner])]
        if not last:
            held = (held[2:] + near_side[2:]) + (across[1:] + corner[1:])
    return tail(cluster_order, near_t, flat_bases, matrices, features, first, mixed, arrivals)


def solution(mesh):
    in_specs = (P("leaf", None), P(None, "leaf"), P("leaf", None), P(None, None, "leaf"), P())
    out_specs = P("leaf", None)
    return jax.shard_map(local, mesh=mesh, in_specs=in_specs, out_specs=out_specs, check_vma=False)
```
